256 devices in a mesh: step: 32 (over y, z), ex: 8 (over x, core).
Axes of the slice: x: 4, y: 4, z: 8, core: 2. Of those that a mesh axis runs over, the one named last changes fastest.
Arguments:
- gradients: bfloat16 [256, 1024, 512], P('step', 'ex'), may hold values from -6 to 6, as said below
- step_rates: float32 [256], P('step'), may hold values from 0.02 to 0.08
Outputs:
- embeddings: float32 [256, 1024, 512], P('step', 'ex')
The draws below stay inside these ranges and needn't reach their ends.
Inputs may be any that keep to these rules, and one draw needn't show every extreme that they name: real-valued projected gradients.
All inputs are finite; a program needn't handle non-finite values.
Results may differ from the reference program's by a relative error of at most 0.0003.
Values may be sent and summed in bfloat16 or wider, within the bound.
A program may use at most 128 MiB of HBM per device.

```python
import math
import jax
import jax.numpy as jnp
from jax import lax

P_SIZE = 512
BATCH = 1024
STEPS = 256


def draw_gradients(key, part):
    key = jax.random.fold_in(key, 11)
    shape = (STEPS, BATCH, P_SIZE)
    return jax.random.truncated_normal(key, -6.0, 6.0, shape, jnp.float32).astype(jnp.bfloat16)


def levels(rng, shape, cuts, least, largest):
    def one(axis_at, parts):
        steps = jax.random.uniform(jax.random.fold_in(jax.random.fold_in(rng, 6), axis_at), (parts,), jnp.float32, least / len(cuts), largest / len(cuts))
        return jnp.repeat(jnp.exp(steps), shape[axis_at] // parts).reshape((-1,) + (1,) * (len(shape) - axis_at - 1))

    loudness = one(*cuts[0])
    for cut in cuts[1:]:
        loudness = loudness * one(*cut)
    return loudness


def setup_inputs(seed: int = 0) -> dict:
    keys = jax.random.split(jax.random.key(seed), 3)
    return {
        "gradients": draw_gradients(jax.random.fold_in(keys[2], 71), 0),
        "step_rates": jnp.clip(jnp.exp(math.log(0.08) - 1.3862944 * jax.random.uniform(keys[1], (STEPS,), jnp.float32) ** levels(keys[1], (STEPS,), ((0, 32),), -0.2, 0.2)), 0.02, 0.08),
    }


def reference(gradients, step_rates):
    spectral_edge = (math.sqrt(BATCH) + math.sqrt(P_SIZE)) ** 2
    identity = jnp.eye(P_SIZE, dtype=jnp.float32)

    def one_step(outer_region, inputs):
        example_rows, step_rate = inputs
        broad_row_matrix = example_rows.astype(jnp.float32)
        embedded = jnp.dot(broad_row_matrix, outer_region.T, precision=lax.Precision.HIGHEST)
        inner_products = jnp.dot(example_rows.T, example_rows, preferred_element_type=jnp.float32)
        step_map = identity - step_rate / spectral_edge * inner_products
        return (jnp.dot(outer_region, step_map, precision=lax.Precision.HIGHEST), embedded)
    final_product, embeddings = lax.scan(one_step, identity, (gradients, step_rates), reverse=True)
    return embeddings
```

```python
import functools
import math

import jax
import jax.numpy as jnp
from jax import lax
from jax.experimental import pallas as pl
from jax.experimental.pallas import tpu as pltpu
from jax.sharding import PartitionSpec as P

P_SIZE = 512
BATCH = 1024
NX, NY, NZ = 4, 4, 8
STEPS_HERE = 8
EX_HERE = 128
TILE = 128
ABOVE = [(a, b) for a in range(4) for b in range(a + 1, 4)]
PAIRS = [(0, 1), (2, 3)]
PACK = 16 + (len(ABOVE) + len(PAIRS)) * TILE
CUT = PACK // 4 // 16 * 16
PARTS = ((0, CUT), (CUT, CUT), (2 * CUT, CUT), (3 * CUT, PACK - 3 * CUT))
PIECE = 64
F32, BF16 = jnp.float32, jnp.bfloat16
MESH = pl.DeviceIdType.MESH


def dot_nn(a, b):
    return lax.dot_general(a, b, (((1,), (0,)), ((), ())), preferred_element_type=F32)


def dot_tn(a, b):
    return lax.dot_general(a, b, (((0,), (0,)), ((), ())), preferred_element_type=F32)


def two_parts(v):
    hi = v.astype(BF16)
    return hi, (v - hi.astype(F32)).astype(BF16)


def eye_mask(rows, columns, row0):
    r = lax.broadcasted_iota(jnp.int32, (rows, columns), 0) + row0
    return r == lax.broadcasted_iota(jnp.int32, (rows, columns), 1)


def times_rows(x, diag, off_ref):
    n = x.shape[0]
    y = dot_nn(jnp.concatenate(two_parts(x), axis=0), off_ref[...])
    return x * diag + (y[:n] + y[n:])


def rows_plus_diag(diag, off_ref, start, n):
    return off_ref[pl.ds(start, n), :].astype(F32) + jnp.where(eye_mask(n, P_SIZE, start), diag, 0.0)


def rows_less_diag(x, diag, start):
    return (x - jnp.where(eye_mask(x.shape[0], P_SIZE, start), diag, 0.0)).astype(BF16)


def apply_part(x_ref, diag, off_ref, at, count):
    x = x_ref[pl.ds(at, count)].reshape(count * EX_HERE, P_SIZE)
    x = x * diag + dot_nn(x.astype(BF16), off_ref[...])
    x_ref[pl.ds(at, count)] = x.reshape(count, EX_HERE, P_SIZE)


def loop(first, last, run):
    def one(i, _):
        run(i)
        return 0

    lax.fori_loop(first, last, one, 0)


def choose(k, table):
    value = table[0]
    for i in range(1, len(table)):
        value = jnp.where(k == i, table[i], value)
    return value


def body(g_hbm, rate_hbm, out_ref, g_ref, rate_ref, gather, stage_r, stage_l, pack, maps, diags, v,
         mine, blocks, block_diags, mine_t, lines, line_diags,
         in_sem, g_send, g_recv, st_recv, p_send, p_recv,
         b_send, b_recv, bd_send, bd_recv, t_send, t_recv, td_send, td_recv):
    step, ex = lax.axis_index("step"), lax.axis_index("ex")
    y, z = step // NZ, step % NZ
    x, c = ex // 2, ex % 2
    xr, xl, xo = (x + 1) % NX, (x + 3) % NX, (x + 2) % NX
    sib = (step, x * 2 + 1 - c)
    right, left = (step, xr * 2 + c), (step, xl * 2 + c)
    z_next, z_prev = (y * NZ + (z + 1) % NZ, ex), (y * NZ + (z + NZ - 1) % NZ, ex)
    y_next, y_prev = (((y + 1) % NY) * NZ + z, ex), (((y + NY - 1) % NY) * NZ + z, ex)

    barrier = pltpu.get_barrier_semaphore()
    peers = [sib, right, left, (step, xr * 2 + 1 - c), (step, xl * 2 + 1 - c), z_next, z_prev, y_next, y_prev]
    for peer in peers:
        pl.semaphore_signal(barrier, inc=1, device_id=peer, device_id_type=MESH)
    pl.semaphore_wait(barrier, len(peers))

    def remote(src, dst, send, recv, device):
        return pltpu.make_async_remote_copy(
            src_ref=src, dst_ref=dst, send_sem=send, recv_sem=recv, device_id=device, device_id_type=MESH
        )

    started = []

    def go(copy):
        copy.start()
        started.append(copy)

    half = EX_HERE // 2

    def send_set(core):
        n = 1 + core * 6
        step_o, step_r, step_l = xo * 2 + core, xr * 2 + core, xl * 2 + core
        go(remote(g_hbm.at[step_o, pl.ds(0, half), :], stage_r.at[core], g_send.at[n], st_recv.at[core, 0], right))
        go(remote(g_hbm.at[step_o, pl.ds(half, half), :], stage_l.at[core], g_send.at[n + 1], st_recv.at[core, 1],
                  left))
        go(remote(g_hbm.at[step_r], gather.at[ex], g_send.at[n + 2], g_recv.at[ex, 0], (step, step_r)))
        go(remote(g_hbm.at[step_l], gather.at[ex], g_send.at[n + 3], g_recv.at[ex, 0], (step, step_l)))

    def forward_set(core):
        n = 1 + core * 6
        remote(stage_r.at[core], stage_r.at[core], g_send.at[0], st_recv.at[core, 0], sib).wait_recv()
        go(remote(stage_r.at[core], gather.at[xl * 2 + c, pl.ds(0, half), :], g_send.at[n + 4],
                  g_recv.at[xl * 2 + c, 0], (step, xr * 2 + core)))
        remote(stage_l.at[core], stage_l.at[core], g_send.at[0], st_recv.at[core, 1], sib).wait_recv()
        go(remote(stage_l.at[core], gather.at[xr * 2 + c, pl.ds(half, half), :], g_send.at[n + 5],
                  g_recv.at[xr * 2 + c, 1], (step, xl * 2 + core)))

    go(remote(g_hbm.at[x * 2 + 1 - c], gather.at[ex], g_send.at[0], g_recv.at[ex, 0], sib))
    send_set(0)
    own_in = pltpu.make_async_copy(g_hbm.at[ex], gather.at[ex], in_sem.at[0])
    all_in = pltpu.make_async_copy(g_hbm, g_ref, in_sem.at[1])
    rate_in = pltpu.make_async_copy(rate_hbm, rate_ref, in_sem.at[2])
    own_in.start()
    all_in.start()
    rate_in.start()
    forward_set(0)
    send_set(1)
    own_in.wait()
    rate_in.wait()

    def gram_of(chip, first):
        rows = gather[pl.ds(chip * 2, 2)].reshape(2 * EX_HERE, P_SIZE)
        if first:
            v[...] = dot_tn(rows, rows)
        else:
            v[...] += dot_tn(rows, rows)

    def arrived(source):
        remote(gather.at[source], gather.at[source], g_send.at[0], g_recv.at[source, 0], sib).wait_recv()

    def arrived_half(source, which):
        part = gather.at[source, pl.ds(which * half, half), :]
        remote(part, part, g_send.at[0], g_recv.at[source, which], sib).wait_recv()

    def gram_near():
        arrived(x * 2 + 1 - c)
        gram_of(x, True)

    def gram_far():
        for at in (xr, xl):
            for core in range(2):
                arrived(at * 2 + core)
            gram_of(at, False)
        for core in range(2):
            for which in range(2):
                arrived_half(xo * 2 + core, which)
        gram_of(xo, False)

    edge = (math.sqrt(BATCH) + math.sqrt(P_SIZE)) ** 2
    scale = rate_ref[ex] / edge
    own = pack.at[ex]
    row_at = lax.broadcasted_iota(jnp.int32, (TILE, TILE), 0)
    column_at = lax.broadcasted_iota(jnp.int32, (TILE, TILE), 1)
    on, upper, lower = row_at == column_at, row_at < column_at, row_at > column_at

    def pack_map():
        def map_tile(a, b):
            return v[pl.ds(a * TILE, TILE), pl.ds(b * TILE, TILE)] * (-scale)

        diag_parts = []
        for a in range(4):
            d = 1.0 + jnp.sum(jnp.where(on, map_tile(a, a), 0.0), axis=0, keepdims=True)
            d_hi, d_rest = d.astype(BF16).astype(F32), d - d.astype(BF16).astype(F32)
            d_mid = d_rest.astype(BF16).astype(F32)
            diag_parts.append((d_hi, d_mid, d_rest - d_mid))
        for n, (a, b) in enumerate(ABOVE):
            own[pl.ds(16 + n * TILE, TILE), :] = map_tile(a, b).astype(BF16)
        for n, (a, b) in enumerate(PAIRS):
            both = jnp.where(upper, map_tile(a, a), jnp.where(lower, map_tile(b, b), 0.0))
            own[pl.ds(16 + (len(ABOVE) + n) * TILE, TILE), :] = both.astype(BF16)
        rows = [diag_parts[a][part] for part in range(3) for a in range(4)]
        own[pl.ds(0, 16), :] = jnp.concatenate(rows + [jnp.zeros((4, TILE), F32)], axis=0).astype(BF16)

    def packed(slot, which):
        at, size = (0, PACK) if which == 4 else PARTS[which]
        return pack.at[slot, pl.ds(at, size), :]

    p_count = [0]

    def send_pack(slot, which, device):
        n = p_count[0]
        p_count[0] += 1
        go(remote(packed(slot, which), packed(slot, which), p_send.at[n], p_recv.at[slot, which], device))

    def got_pack(slot, which):
        remote(packed(slot, which), packed(slot, which), p_send.at[0], p_recv.at[slot, which], sib).wait_recv()

    def unpack(slot):
        parts = pack[slot, pl.ds(0, 16), :].astype(F32)
        diag = parts[0:4] + (parts[4:8] + parts[8:12])
        for a in range(4):
            diags[slot, :, pl.ds(a * TILE, TILE)] = diag[a:a + 1]

        def put(a, b, tile):
            maps[slot, pl.ds(a * TILE, TILE), pl.ds(b * TILE, TILE)] = tile

        for n, (a, b) in enumerate(ABOVE):
            tile = pack[slot, pl.ds(16 + n * TILE, TILE), :]
            put(a, b, tile)
            put(b, a, tile.T)
        for n, (a, b) in enumerate(PAIRS):
            tile = pack[slot, pl.ds(16 + (len(ABOVE) + n) * TILE, TILE), :].astype(F32)
            turned = tile.T
            put(a, a, jnp.where(upper, tile, turned).astype(BF16))
            put(b, b, jnp.where(lower, tile, turned).astype(BF16))

    first = []
    for which, device in ((0, left), (2, right), (1, left), (3, right), (2, left), (0, right), (3, left), (1, right),
                          (4, sib)):
        n = len(first)
        first.append(remote(packed(ex, which), packed(ex, which), p_send.at[n], p_recv.at[ex, which], device))
    p_count[0] = len(first)

    def send_first():
        for copy in first:
            copy.start()

    @pl.when(c == 0)
    def _():
        gram_near()
        gram_far()
        pack_map()

    @pl.when(c == 1)
    def _():
        gram_near()

    forward_set(1)

    @pl.when(c == 0)
    def _():
        send_first()

    @pl.when(c == 1)
    def _():
        gram_far()
        pack_map()
        send_first()

    started.extend(first)
    all_in.wait()
    from_right, from_left, across = xr * 2 + c, xl * 2 + c, xo * 2 + c
    unpack(ex)
    for s in range(STEPS_HERE):
        out_ref[s] = g_ref[s].astype(F32)

    def take(chip):
        got_pack(chip * 2 + 1 - c, 4)
        unpack(chip * 2 + 1 - c)

    @pl.when(c == 1)
    def _():
        take(x)

    def both(slot, which, device, device_0):
        send_pack(slot, which, device)
        n = p_count[0]
        p_count[0] += 1
        copy = remote(packed(slot, which), packed(slot, which), p_send.at[n], p_recv.at[slot, which], device_0)
        extra.append(copy)

        @pl.when(c == 1)
        def _():
            copy.start()

    extra = []
    for which in range(2):
        got_pack(from_right, which)
        both(from_right, which, left, (step, xl * 2))
        got_pack(from_left, 2 + which)
        both(from_left, 2 + which, right, (step, xr * 2))
    for which in range(2):
        got_pack(from_right, 2 + which)
        got_pack(from_left, which)
    send_pack(from_right, 4, sib)
    send_pack(from_left, 4, sib)
    unpack(from_right)
    unpack(from_left)

    @pl.when(c == 1)
    def _():
        take(xr)
        take(xl)

    for which in range(4):
        got_pack(across, which)
    over = remote(packed(across, 4), packed(across, 4), p_send.at[p_count[0]], p_recv.at[across, 4], sib)

    @pl.when(c == 0)
    def _():
        over.start()

    unpack(across)

    @pl.when(c == 0)
    def _():
        take(x)
        take(xr)
        take(xl)
        for which in range(4):
            got_pack(xo * 2 + 1, which)

    @pl.when(c == 1)
    def _():
        got_pack(xo * 2, 4)

    unpack(xo * 2 + 1 - c)

    quarters = (x % 2) * 2
    start = pl.multiple_of((c * 4 + quarters) * PIECE, 2 * PIECE)
    few = rows_plus_diag(diags[0], maps.at[0], start, 2 * PIECE)
    for s in range(1, STEPS_HERE):
        few = times_rows(few, diags[s], maps.at[s])
    block_diag = diags[0]
    for s in range(1, STEPS_HERE):
        block_diag = block_diag * diags[s]
    block_diags[z] = block_diag
    mine[...] = rows_less_diag(few, block_diag, start)
    blocks[z, pl.ds(start, 2 * PIECE), :] = mine[...]

    def single(j):
        apply_part(out_ref, diags[j * 2 + 1], maps.at[j * 2 + 1], j * 2, 1)

    def unit(u):
        s = choose(u, (2, 3, 4, 4, 5, 5, 6, 6, 6, 7, 7, 7))
        pair = choose(u, (0, 0, 0, 1, 0, 1, 0, 1, 2, 0, 1, 2))
        apply_part(out_ref, diags[s], maps.at[s], pair * 2, 2)

    def later(u):
        slot = z + 1 + u // 4
        apply_part(out_ref, block_diags[slot], blocks.at[slot], (u % 4) * 2, 2)

    units = 4 * (NZ - 1 - z)

    def later_units(first, last):
        loop(jnp.minimum(first, units), jnp.minimum(last, units), later)

    early = z < NZ // 2
    inner_done = jnp.where(early, 12, 5)

    def ring(own, buf, dbuf, n, pos, ahead, behind, send, recv, d_send, d_recv, own_too, before):
        a_at = jnp.where(x == 3, 1, 0)
        to_left = jnp.where(x == 1, 0, 1)
        base = c * 4 + quarters
        p_a, p_b = base + a_at, base + 1 - a_at
        turns = n // 2

        def rows(slot, at, count):
            return buf.at[slot, pl.ds(pl.multiple_of(at * PIECE, PIECE), count * PIECE), :]

        def pass_on(slot, at, count, kind, land, device, src=None):
            there = rows(slot, at, count)
            go(remote(there if src is None else src, there, send.at[slot, kind], recv.at[slot, land], device))

        def got(slot, at, count, land):
            there = rows(slot, at, count)
            remote(there, there, send.at[slot, 0], recv.at[slot, land], sib).wait_recv()

        def pass_diag(slot, kind, device):
            go(remote(dbuf.at[slot], dbuf.at[slot], d_send.at[slot, kind], d_recv.at[slot], device))

        def got_diag(slot):
            remote(dbuf.at[slot], dbuf.at[slot], d_send.at[slot, 0], d_recv.at[slot], sib).wait_recv()

        def part(src, at):
            return None if src is None else src.at[pl.ds(pl.multiple_of(at * PIECE, PIECE), PIECE), :]

        def left_copy(slot, src=None):
            there = rows(slot, base + to_left, 1)
            mine_there = part(src, to_left)
            return remote(there if src is None else mine_there, there, send.at[slot, 5],
                          recv.at[slot, 2 + to_left], left)

        def over_a(slot, src=None):
            pass_on(slot, p_a, 1, 4, 2 + a_at, right, part(src, a_at))
            copy = left_copy(slot, src)

            @pl.when(x % 2 == 1)
            def _():
                copy.start()

            started.append(copy)

        def over_b(slot, src=None):
            copy = left_copy(slot, src)

            @pl.when(x % 2 == 0)
            def _():
                copy.start()

        def to_sibling(slot, src=None):
            pass_on(slot, base, 2, 6, 4, sib, src)

        other = c * 4 + 2 - quarters

        def over_x(slot):
            got(slot, other, 1, 2)
            got(slot, other + 1, 1, 3)
            pass_on(slot, other, 2, 7, 5, sib)

        def got_all(slot):
            got(slot, (1 - c) * 4 + quarters, 2, 4)
            got(slot, (1 - c) * 4 + 2 - quarters, 2, 5)

        own_a, own_b = part(own, a_at), part(own, 1 - a_at)
        pass_on(pos, p_a, 1, 0, 0, ahead, own_a)
        pass_on(pos, p_b, 1, 3, 1, behind, own_b)
        pass_on(pos, p_b, 1, 1, 1, ahead, own_b)
        pass_on(pos, p_a, 1, 2, 0, behind, own_a)
        pass_diag(pos, 0, ahead)
        pass_diag(pos, 1, behind)
        if own_too:
            over_a(pos, own)
            over_b(pos, own)
            to_sibling(pos, own)

        waiting = [pos] if own_too else []
        for s in range(turns):
            last = s == turns - 1
            up, down = (pos + n - 1 - s) % n, (pos + 1 + s) % n
            before[s](got_all)
            got(up, p_a, 1, 0)
            if not last:
                pass_on(up, p_a, 1, 0, 0, ahead)
            over_a(up)
            got(down, p_b, 1, 1)
            if not last:
                pass_on(down, p_b, 1, 3, 1, behind)
            over_b(down)
            if last:
                to_sibling(up)
            else:
                got(up, p_b, 1, 1)
                if s < turns - 2:
                    pass_on(up, p_b, 1, 1, 1, ahead)
                over_b(up)
                got(down, p_a, 1, 0)
                if s < turns - 2:
                    pass_on(down, p_a, 1, 2, 0, behind)
                over_a(down)
                to_sibling(up)
                to_sibling(down)
            got_diag(up)
            if not last:
                pass_diag(up, 0, ahead)
                got_diag(down)
                if s < turns - 2:
                    pass_diag(down, 1, behind)
            for slot in waiting:
                over_x(slot)
            waiting = [up] if last else [up, down]
        before[turns](got_all)
        for slot in waiting:
            over_x(slot)

        return got_all

    def first_fill(got_all):
        loop(0, STEPS_HERE // 2, single)
        loop(0, inner_done, unit)

    def block_fill(d):
        def run(got_all):
            got_all((z + d) % NZ)

            @pl.when(early)
            def _():
                loop(4 * d - 4, 4 * d, later)

        return run

    def last_fill(got_all):
        got_all((z + 3) % NZ)
        for d in (0, 5, 6, 7):
            got_all((z + d) % NZ)

        @pl.when(early)
        def _():
            loop(8, 12, later)

    got_all = ring(mine, blocks, block_diags, NZ, z, z_next, z_prev, b_send, b_recv, bd_send, bd_recv, True,
                   [first_fill, lambda _: None, block_fill(1), block_fill(2), last_fill])

    farthest = (z + NZ // 2) % NZ

    @pl.when(z >= NZ // 2)
    def _():
        got_all(farthest)

    few = rows_plus_diag(block_diags[0], blocks.at[0], start, 2 * PIECE)
    for s in range(1, NZ // 2):
        few = times_rows(few, block_diags[s], blocks.at[s])

    @pl.when(early)
    def _():
        got_all(farthest)

    for s in range(NZ // 2, NZ):
        few = times_rows(few, block_diags[s], blocks.at[s])
    line_diag = block_diags[0]
    for s in range(1, NZ):
        line_diag = line_diag * block_diags[s]
    line_diags[y] = line_diag
    mine_t[...] = rows_less_diag(few, line_diag, start)

    done = jnp.where(early, 12, 0)

    def line_fill(got_all):
        loop(inner_done, 12, unit)
        later_units(done, done + 8)

    got_all = ring(mine_t, lines, line_diags, NY, y, y_next, y_prev, t_send, t_recv, td_send, td_recv, False,
                   [line_fill, lambda _: later_units(done + 8, done + 12), lambda _: None])
    later_units(done + 12, done + 28)

    for d in range(1, NY):
        got_all((y + d) % NY)

        @pl.when(y + d < NY)
        def _():
            for at in (0, 4):
                apply_part(out_ref, line_diags[(y + d) % NY], lines.at[(y + d) % NY], at, 4)

    for copy in started:
        copy.wait_send()

    @pl.when(c == 1)
    def _():
        for copy in extra:
            copy.wait_send()

    @pl.when(c == 0)
    def _():
        over.wait_send()


def per_device(gradients, step_rates):
    square = (P_SIZE, P_SIZE)
    dma = pltpu.SemaphoreType.DMA
    return pl.pallas_call(
        body,
        out_shape=jax.ShapeDtypeStruct(gradients.shape, F32),
        in_specs=[pl.BlockSpec(memory_space=pl.ANY)] * 2,
        out_specs=pl.BlockSpec(memory_space=pltpu.VMEM),
        scratch_shapes=[
            pltpu.VMEM((STEPS_HERE, EX_HERE, P_SIZE), BF16),
            pltpu.SMEM((STEPS_HERE,), F32),
            pltpu.VMEM((8, EX_HERE, P_SIZE), BF16),
            pltpu.VMEM((2, EX_HERE // 2, P_SIZE), BF16),
            pltpu.VMEM((2, EX_HERE // 2, P_SIZE), BF16),
            pltpu.VMEM((STEPS_HERE, PACK, TILE), BF16),
            pltpu.VMEM((STEPS_HERE,) + square, BF16),
            pltpu.VMEM((STEPS_HERE, 1, P_SIZE), F32),
            pltpu.VMEM(square, F32),
            pltpu.VMEM((2 * PIECE, P_SIZE), BF16),
            pltpu.VMEM((NZ,) + square, BF16),
            pltpu.VMEM((NZ, 1, P_SIZE), F32),
            pltpu.VMEM((2 * PIECE, P_SIZE), BF16),
            pltpu.VMEM((NY,) + square, BF16),
            pltpu.VMEM((NY, 1, P_SIZE), F32),
            dma((3,)),
            dma((13,)), dma((8, 2)), dma((2, 2)), dma((20,)), dma((8, 5)),
            dma((NZ, 8)), dma((NZ, 6)), dma((NZ, 2)), dma((NZ,)),
            dma((NY, 8)), dma((NY, 6)), dma((NY, 2)), dma((NY,)),
        ],
        compiler_params=pltpu.CompilerParams(
            collective_id=0, has_side_effects=True, vmem_limit_bytes=48 * 1024 * 1024
        ),
    )(pltpu.with_memory_space_constraint(gradients, pltpu.HBM),
      pltpu.with_memory_space_constraint(step_rates, pltpu.HBM))


def solution(mesh):
    in_specs = (P("step", "ex", None), P("step"))
    out_specs = P("step", "ex", None)
    return jax.shard_map(
        per_device, mesh=mesh, in_specs=in_specs, out_specs=out_specs, check_vma=False
    )
```

```python
import functools
import math

import jax
import jax.numpy as jnp
from jax import lax
from jax.experimental import pallas as pl
from jax.experimental.pallas import tpu as pltpu
from jax.sharding import PartitionSpec as P

P_SIZE = 512
BATCH = 1024
NX, NY, NZ = 4, 4, 8
STEPS_HERE = 8
EX_HERE = 128
TILE = 128
ABOVE = [(a, b) for a in range(4) for b in range(a + 1, 4)]
PAIRS = [(0, 1), (2, 3)]
PACK = 16 + (len(ABOVE) + len(PAIRS)) * TILE
CUT = PACK // 2 // 16 * 16
PARTS = ((0, CUT), (CUT, PACK - CUT))
PIECE = 64
F32, BF16 = jnp.float32, jnp.bfloat16
MESH = pl.DeviceIdType.MESH


def dot_nn(a, b):
    return lax.dot_general(a, b, (((1,), (0,)), ((), ())), preferred_element_type=F32)


def dot_tn(a, b):
    return lax.dot_general(a, b, (((0,), (0,)), ((), ())), preferred_element_type=F32)


def two_parts(v):
    hi = v.astype(BF16)
    return hi, (v - hi.astype(F32)).astype(BF16)


def eye_mask(rows, columns, row0):
    r = lax.broadcasted_iota(jnp.int32, (rows, columns), 0) + row0
    return r == lax.broadcasted_iota(jnp.int32, (rows, columns), 1)


def times_rows(x_ref, diag, off_ref):
    x = x_ref[...]
    n = x.shape[0]
    y = dot_nn(jnp.concatenate(two_parts(x), axis=0), off_ref[...])
    x_ref[...] = x * diag + (y[:n] + y[n:])


def rows_plus_diag(x_ref, diag, off_ref, start):
    n = x_ref.shape[0]
    x_ref[...] = off_ref[pl.ds(start, n), :].astype(F32) + jnp.where(eye_mask(n, P_SIZE, start), diag, 0.0)


def rows_less_diag(x_ref, diag, off_ref, start):
    x = x_ref[...]
    off_ref[...] = (x - jnp.where(eye_mask(x.shape[0], P_SIZE, start), diag, 0.0)).astype(BF16)


def apply_part(x_ref, diag, off_ref, at, count):
    x = x_ref[pl.ds(at, count)].reshape(count * EX_HERE, P_SIZE)
    x = x * diag + dot_nn(x.astype(BF16), off_ref[...])
    x_ref[pl.ds(at, count)] = x.reshape(count, EX_HERE, P_SIZE)


def loop(first, last, run):
    def one(i, _):
        run(i)
        return 0

    lax.fori_loop(first, last, one, 0)


def choose(k, table):
    value = table[0]
    for i in range(1, len(table)):
        value = jnp.where(k == i, table[i], value)
    return value


def body(g_hbm, rate_hbm, out_ref, last_ref, last_diag, g_ref, rate_ref, gather, stage_r, stage_l, pack, maps, diags, v,
         few, mine, blocks, block_diags, mine_t, lines, line_diags,
         in_sem, g_send, g_recv, st_recv, p_send, p_recv,
         b_send, b_recv, bd_send, bd_recv, t_send, t_recv, td_send, td_recv):
    step, ex = lax.axis_index("step"), lax.axis_index("ex")
    y, z = step // NZ, step % NZ
    x, c = ex // 2, ex % 2
    xr, xl, xo = (x + 1) % NX, (x + 3) % NX, (x + 2) % NX
    sib = (step, x * 2 + 1 - c)
    right, left = (step, xr * 2 + c), (step, xl * 2 + c)
    z_next, z_prev = (y * NZ + (z + 1) % NZ, ex), (y * NZ + (z + NZ - 1) % NZ, ex)
    y_next, y_prev = (((y + 1) % NY) * NZ + z, ex), (((y + NY - 1) % NY) * NZ + z, ex)

    barrier = pltpu.get_barrier_semaphore()
    peers = [sib, right, left, (step, xr * 2 + 1 - c), (step, xl * 2 + 1 - c), z_next, z_prev, y_next, y_prev]
    for peer in peers:
        pl.semaphore_signal(barrier, inc=1, device_id=peer, device_id_type=MESH)
    pl.semaphore_wait(barrier, len(peers))

    def remote(src, dst, send, recv, device):
        return pltpu.make_async_remote_copy(
            src_ref=src, dst_ref=dst, send_sem=send, recv_sem=recv, device_id=device, device_id_type=MESH
        )

    started = []

    def go(copy):
        copy.start()
        started.append(copy)

    half = EX_HERE // 2

    def send_set(core):
        n = 1 + core * 6
        step_o, step_r, step_l = xo * 2 + core, xr * 2 + core, xl * 2 + core
        go(remote(g_hbm.at[step_o, pl.ds(0, half), :], stage_r.at[core], g_send.at[n], st_recv.at[core, 0], right))
        go(remote(g_hbm.at[step_o, pl.ds(half, half), :], stage_l.at[core], g_send.at[n + 1], st_recv.at[core, 1],
                  left))
        go(remote(g_hbm.at[step_r], gather.at[ex], g_send.at[n + 2], g_recv.at[ex, 0], (step, step_r)))
        go(remote(g_hbm.at[step_l], gather.at[ex], g_send.at[n + 3], g_recv.at[ex, 0], (step, step_l)))

    def forward_set(core):
        n = 1 + core * 6
        remote(stage_r.at[core], stage_r.at[core], g_send.at[0], st_recv.at[core, 0], sib).wait_recv()
        go(remote(stage_r.at[core], gather.at[xl * 2 + c, pl.ds(0, half), :], g_send.at[n + 4],
                  g_recv.at[xl * 2 + c, 0], (step, xr * 2 + core)))
        remote(stage_l.at[core], stage_l.at[core], g_send.at[0], st_recv.at[core, 1], sib).wait_recv()
        go(remote(stage_l.at[core], gather.at[xr * 2 + c, pl.ds(half, half), :], g_send.at[n + 5],
                  g_recv.at[xr * 2 + c, 1], (step, xl * 2 + core)))

    go(remote(g_hbm.at[x * 2 + 1 - c], gather.at[ex], g_send.at[0], g_recv.at[ex, 0], sib))
    send_set(0)
    own_in = pltpu.make_async_copy(g_hbm.at[ex], gather.at[ex], in_sem.at[0])
    all_in = pltpu.make_async_copy(g_hbm, g_ref, in_sem.at[1])
    rate_in = pltpu.make_async_copy(rate_hbm, rate_ref, in_sem.at[2])
    own_in.start()
    all_in.start()
    rate_in.start()
    forward_set(0)
    send_set(1)
    own_in.wait()
    rate_in.wait()

    def gram_of(chip, first):
        rows = gather[pl.ds(chip * 2, 2)].reshape(2 * EX_HERE, P_SIZE)
        if first:
            v[...] = dot_tn(rows, rows)
        else:
            v[...] += dot_tn(rows, rows)

    def arrived(source):
        remote(gather.at[source], gather.at[source], g_send.at[0], g_recv.at[source, 0], sib).wait_recv()

    def arrived_half(source, which):
        part = gather.at[source, pl.ds(which * half, half), :]
        remote(part, part, g_send.at[0], g_recv.at[source, which], sib).wait_recv()

    def gram_near():
        arrived(x * 2 + 1 - c)
        gram_of(x, True)

    def gram_far():
        for at in (xr, xl):
            for core in range(2):
                arrived(at * 2 + core)
            gram_of(at, False)
        for core in range(2):
            for which in range(2):
                arrived_half(xo * 2 + core, which)
        gram_of(xo, False)

    edge = (math.sqrt(BATCH) + math.sqrt(P_SIZE)) ** 2
    scale = rate_ref[ex] / edge
    own = pack.at[ex]
    row_at = lax.broadcasted_iota(jnp.int32, (TILE, TILE), 0)
    column_at = lax.broadcasted_iota(jnp.int32, (TILE, TILE), 1)
    on, upper, lower = row_at == column_at, row_at < column_at, row_at > column_at

    def pack_map():
        def map_tile(a, b):
            return v[pl.ds(a * TILE, TILE), pl.ds(b * TILE, TILE)] * (-scale)

        diag_parts = []
        for a in range(4):
            d = 1.0 + jnp.sum(jnp.where(on, map_tile(a, a), 0.0), axis=0, keepdims=True)
            d_hi, d_rest = d.astype(BF16).astype(F32), d - d.astype(BF16).astype(F32)
            d_mid = d_rest.astype(BF16).astype(F32)
            diag_parts.append((d_hi, d_mid, d_rest - d_mid))
        for n, (a, b) in enumerate(ABOVE):
            own[pl.ds(16 + n * TILE, TILE), :] = map_tile(a, b).astype(BF16)
        for n, (a, b) in enumerate(PAIRS):
            both = jnp.where(upper, map_tile(a, a), jnp.where(lower, map_tile(b, b), 0.0))
            own[pl.ds(16 + (len(ABOVE) + n) * TILE, TILE), :] = both.astype(BF16)
        rows = [diag_parts[a][part] for part in range(3) for a in range(4)]
        own[pl.ds(0, 16), :] = jnp.concatenate(rows + [jnp.zeros((4, TILE), F32)], axis=0).astype(BF16)

    def packed(slot, which):
        at, size = (0, PACK) if which == 2 else PARTS[which]
        return pack.at[slot, pl.ds(at, size), :]

    p_count = [0]

    def send_pack(slot, which, device):
        n = p_count[0]
        p_count[0] += 1
        go(remote(packed(slot, which), packed(slot, which), p_send.at[n], p_recv.at[slot, which], device))

    def got_pack(slot, which):
        remote(packed(slot, which), packed(slot, which), p_send.at[0], p_recv.at[slot, which], sib).wait_recv()

    def unpack(slot):
        parts = pack[slot, pl.ds(0, 16), :].astype(F32)
        diag = parts[0:4] + (parts[4:8] + parts[8:12])
        for a in range(4):
            diags[slot, :, pl.ds(a * TILE, TILE)] = diag[a:a + 1]

        def put(a, b, tile):
            maps[slot, pl.ds(a * TILE, TILE), pl.ds(b * TILE, TILE)] = tile

        for n, (a, b) in enumerate(ABOVE):
            tile = pack[slot, pl.ds(16 + n * TILE, TILE), :]
            put(a, b, tile)
            put(b, a, tile.T)
        for n, (a, b) in enumerate(PAIRS):
            tile = pack[slot, pl.ds(16 + (len(ABOVE) + n) * TILE, TILE), :].astype(F32)
            turned = tile.T
            put(a, a, jnp.where(upper, tile, turned).astype(BF16))
            put(b, b, jnp.where(lower, tile, turned).astype(BF16))

    first = []
    for which, device in ((0, left), (1, right), (1, left), (0, right), (2, sib)):
        n = len(first)
        first.append(remote(packed(ex, which), packed(ex, which), p_send.at[n], p_recv.at[ex, which], device))
    p_count[0] = len(first)

    def send_first():
        for copy in first:
            copy.start()

    @pl.when(c == 0)
    def _():
        gram_near()
        gram_far()
        pack_map()

    @pl.when(c == 1)
    def _():
        gram_near()

    forward_set(1)

    @pl.when(c == 0)
    def _():
        send_first()

    @pl.when(c == 1)
    def _():
        gram_far()
        pack_map()
        send_first()

    started.extend(first)
    all_in.wait()
    from_right, from_left, across = xr * 2 + c, xl * 2 + c, xo * 2 + c
    unpack(ex)
    for s in range(STEPS_HERE):
        out_ref[s] = g_ref[s].astype(F32)

    def take(chip):
        got_pack(chip * 2 + 1 - c, 2)
        unpack(chip * 2 + 1 - c)

    @pl.when(c == 1)
    def _():
        take(x)

    got_pack(from_right, 0)
    send_pack(from_right, 0, left)
    got_pack(from_left, 1)
    send_pack(from_left, 1, right)
    got_pack(from_right, 1)
    send_pack(from_right, 2, sib)
    got_pack(from_left, 0)
    send_pack(from_left, 2, sib)
    unpack(from_right)
    unpack(from_left)

    @pl.when(c == 1)
    def _():
        take(xr)
        take(xl)

    for which in range(2):
        got_pack(across, which)
    send_pack(across, 2, sib)
    unpack(across)

    @pl.when(c == 0)
    def _():
        take(x)
        take(xr)
        take(xl)

    take(xo)

    quarters = (x % 2) * 2
    start = pl.multiple_of((c * 4 + quarters) * PIECE, 2 * PIECE)
    rows_plus_diag(few, diags[0], maps.at[0], start)
    for s in range(1, STEPS_HERE):
        times_rows(few, diags[s], maps.at[s])
    block_diag = diags[0]
    for s in range(1, STEPS_HERE):
        block_diag = block_diag * diags[s]
    block_diags[z] = block_diag
    rows_less_diag(few, block_diag, mine, start)
    blocks[z, pl.ds(start, 2 * PIECE), :] = mine[...]

    def single(j):
        apply_part(out_ref, diags[j * 2 + 1], maps.at[j * 2 + 1], j * 2, 1)

    def unit(u):
        s = choose(u, (2, 3, 4, 4, 5, 5, 6, 6, 6, 7, 7, 7))
        pair = choose(u, (0, 0, 0, 1, 0, 1, 0, 1, 2, 0, 1, 2))
        apply_part(out_ref, diags[s], maps.at[s], pair * 2, 2)

    def later(u):
        slot = z + 1 + u // 4
        apply_part(out_ref, block_diags[slot], blocks.at[slot], (u % 4) * 2, 2)

    units = 4 * (NZ - 1 - z)

    def later_units(first, last):
        loop(jnp.minimum(first, units), jnp.minimum(last, units), later)

    early = z < NZ // 2
    inner_done = jnp.where(early, 12, 5)

    def ring(own, buf, dbuf, n, pos, ahead, behind, send, recv, d_send, d_recv, own_too, before):
        a_at = jnp.where(x == 3, 1, 0)
        to_left = jnp.where(x == 1, 0, 1)
        base = c * 4 + quarters
        p_a, p_b = base + a_at, base + 1 - a_at
        turns = n // 2

        def rows(slot, at, count):
            return buf.at[slot, pl.ds(pl.multiple_of(at * PIECE, PIECE), count * PIECE), :]

        def pass_on(slot, at, count, kind, land, device, src=None):
            there = rows(slot, at, count)
            go(remote(there if src is None else src, there, send.at[slot, kind], recv.at[slot, land], device))

        def got(slot, at, count, land):
            there = rows(slot, at, count)
            remote(there, there, send.at[slot, 0], recv.at[slot, land], sib).wait_recv()

        def pass_diag(slot, kind, device):
            go(remote(dbuf.at[slot], dbuf.at[slot], d_send.at[slot, kind], d_recv.at[slot], device))

        def got_diag(slot):
            remote(dbuf.at[slot], dbuf.at[slot], d_send.at[slot, 0], d_recv.at[slot], sib).wait_recv()

        def part(src, at):
            return None if src is None else src.at[pl.ds(pl.multiple_of(at * PIECE, PIECE), PIECE), :]

        def left_copy(slot, src=None):
            there = rows(slot, base + to_left, 1)
            mine_there = part(src, to_left)
            return remote(there if src is None else mine_there, there, send.at[slot, 5],
                          recv.at[slot, 2 + to_left], left)

        def over_a(slot, src=None):
            pass_on(slot, p_a, 1, 4, 2 + a_at, right, part(src, a_at))
            copy = left_copy(slot, src)

            @pl.when(x % 2 == 1)
            def _():
                copy.start()

            started.append(copy)

        def over_b(slot, src=None):
            copy = left_copy(slot, src)

            @pl.when(x % 2 == 0)
            def _():
                copy.start()

        def to_sibling(slot, src=None):
            pass_on(slot, base, 2, 6, 4, sib, src)

        other = c * 4 + 2 - quarters

        def over_x(slot):
            got(slot, other, 1, 2)
            got(slot, other + 1, 1, 3)
            pass_on(slot, other, 2, 7, 5, sib)

        def got_all(slot):
            got(slot, (1 - c) * 4 + quarters, 2, 4)
            got(slot, (1 - c) * 4 + 2 - quarters, 2, 5)

        own_a, own_b = part(own, a_at), part(own, 1 - a_at)
        pass_on(pos, p_a, 1, 0, 0, ahead, own_a)
        pass_on(pos, p_b, 1, 3, 1, behind, own_b)
        pass_on(pos, p_b, 1, 1, 1, ahead, own_b)
        pass_on(pos, p_a, 1, 2, 0, behind, own_a)
        pass_diag(pos, 0, ahead)
        pass_diag(pos, 1, behind)
        if own_too:
            over_a(pos, own)
            over_b(pos, own)
            to_sibling(pos, own)

        waiting = [pos] if own_too else []
        for s in range(turns):
            last = s == turns - 1
            up, down = (pos + n - 1 - s) % n, (pos + 1 + s) % n
            before[s](got_all)
            got(up, p_a, 1, 0)
            if not last:
                pass_on(up, p_a, 1, 0, 0, ahead)
            over_a(up)
            got(down, p_b, 1, 1)
            if not last:
                pass_on(down, p_b, 1, 3, 1, behind)
            over_b(down)
            if last:
                to_sibling(up)
            else:
                got(up, p_b, 1, 1)
                if s < turns - 2:
                    pass_on(up, p_b, 1, 1, 1, ahead)
                over_b(up)
                got(down, p_a, 1, 0)
                if s < turns - 2:
                    pass_on(down, p_a, 1, 2, 0, behind)
                over_a(down)
                to_sibling(up)
                to_sibling(down)
            got_diag(up)
            if not last:
                pass_diag(up, 0, ahead)
                got_diag(down)
                if s < turns - 2:
                    pass_diag(down, 1, behind)
            for slot in waiting:
                over_x(slot)
            waiting = [up] if last else [up, down]
        before[turns](got_all)
        for slot in waiting:
            over_x(slot)

        return got_all

    def first_fill(got_all):
        loop(0, STEPS_HERE // 2, single)
        loop(0, inner_done, unit)

    def block_fill(d):
        def run(got_all):
            got_all((z + d) % NZ)

            @pl.when(early)
            def _():
                loop(4 * d - 4, 4 * d, later)

        return run

    def last_fill(got_all):
        got_all((z + 3) % NZ)
        for d in (0, 5, 6, 7):
            got_all((z + d) % NZ)

        @pl.when(early)
        def _():
            loop(8, 12, later)

    got_all = ring(mine, blocks, block_diags, NZ, z, z_next, z_prev, b_send, b_recv, bd_send, bd_recv, True,
                   [first_fill, lambda _: None, block_fill(1), block_fill(2), last_fill])

    farthest = (z + NZ // 2) % NZ

    @pl.when(z >= NZ // 2)
    def _():
        got_all(farthest)

    rows_plus_diag(few, block_diags[0], blocks.at[0], start)
    for s in range(1, NZ // 2):
        times_rows(few, block_diags[s], blocks.at[s])

    @pl.when(early)
    def _():
        got_all(farthest)

    for s in range(NZ // 2, NZ):
        times_rows(few, block_diags[s], blocks.at[s])
    line_diag = block_diags[0]
    for s in range(1, NZ):
        line_diag = line_diag * block_diags[s]
    line_diags[y] = line_diag
    rows_less_diag(few, line_diag, mine_t, start)

    done = jnp.where(early, 12, 0)

    def line_fill(got_all):
        loop(inner_done, 12, unit)
        later_units(done, done + 8)

    got_all = ring(mine_t, lines, line_diags, NY, y, y_next, y_prev, t_send, t_recv, td_send, td_recv, False,
                   [line_fill, lambda _: later_units(done + 8, done + 12), lambda _: None])
    later_units(done + 12, done + 28)

    for d in range(1, NY):
        slot = (y + d) % NY
        got_all(slot)

        @pl.when(y + d < NY - 1)
        def _():
            for at in (0, 4):
                apply_part(out_ref, line_diags[slot], lines.at[slot], at, 4)

    @pl.when(y < NY - 1)
    def _():
        last_ref[...] = lines[NY - 1]
        last_diag[...] = line_diags[NY - 1]

    @pl.when(y == NY - 1)
    def _():
        last_ref[...] = jnp.zeros_like(last_ref)
        last_diag[...] = jnp.ones_like(last_diag)

    for copy in started:
        copy.wait_send()


def finish(x_ref, off_ref, diag_ref, out_hbm, held, sem):
    copies = []
    for i in range(STEPS_HERE // 2):
        x = x_ref[pl.ds(i * 2, 2)].reshape(2 * EX_HERE, P_SIZE)
        x = x * diag_ref[...] + dot_nn(x.astype(BF16), off_ref[...])
        held[pl.ds(i * 2, 2)] = x.reshape(2, EX_HERE, P_SIZE)
        copies.append(pltpu.make_async_copy(held.at[pl.ds(i * 2, 2)], out_hbm.at[pl.ds(i * 2, 2)], sem.at[i]))
        copies[-1].start()
    for copy in copies:
        copy.wait()


def per_device(gradients, step_rates):
    square = (P_SIZE, P_SIZE)
    dma = pltpu.SemaphoreType.DMA
    rows, last, diag = pl.pallas_call(
        body,
        out_shape=[jax.ShapeDtypeStruct(gradients.shape, F32), jax.ShapeDtypeStruct(square, BF16),
                   jax.ShapeDtypeStruct((1, P_SIZE), F32)],
        in_specs=[pl.BlockSpec(memory_space=pl.ANY)] * 2,
        out_specs=[pl.BlockSpec(memory_space=pltpu.VMEM)] * 3,
        scratch_shapes=[
            pltpu.VMEM((STEPS_HERE, EX_HERE, P_SIZE), BF16),
            pltpu.SMEM((STEPS_HERE,), F32),
            pltpu.VMEM((8, EX_HERE, P_SIZE), BF16),
            pltpu.VMEM((2, EX_HERE // 2, P_SIZE), BF16),
            pltpu.VMEM((2, EX_HERE // 2, P_SIZE), BF16),
            pltpu.VMEM((STEPS_HERE, PACK, TILE), BF16),
            pltpu.VMEM((STEPS_HERE,) + square, BF16),
            pltpu.VMEM((STEPS_HERE, 1, P_SIZE), F32),
            pltpu.VMEM(square, F32),
            pltpu.VMEM((2 * PIECE, P_SIZE), F32),
            pltpu.VMEM((2 * PIECE, P_SIZE), BF16),
            pltpu.VMEM((NZ,) + square, BF16),
            pltpu.VMEM((NZ, 1, P_SIZE), F32),
            pltpu.VMEM((2 * PIECE, P_SIZE), BF16),
            pltpu.VMEM((NY,) + square, BF16),
            pltpu.VMEM((NY, 1, P_SIZE), F32),
            dma((3,)),
            dma((13,)), dma((8, 2)), dma((2, 2)), dma((16,)), dma((8, 5)),
            dma((NZ, 8)), dma((NZ, 6)), dma((NZ, 2)), dma((NZ,)),
            dma((NY, 8)), dma((NY, 6)), dma((NY, 2)), dma((NY,)),
        ],
        compiler_params=pltpu.CompilerParams(
            collective_id=0, has_side_effects=True, vmem_limit_bytes=48 * 1024 * 1024
        ),
    )(pltpu.with_memory_space_constraint(gradients, pltpu.HBM),
      pltpu.with_memory_space_constraint(step_rates, pltpu.HBM))
    return pl.pallas_call(
        finish,
        out_shape=jax.ShapeDtypeStruct(gradients.shape, F32),
        in_specs=[pl.BlockSpec(memory_space=pltpu.VMEM)] * 3,
        out_specs=pl.BlockSpec(memory_space=pl.ANY),
        scratch_shapes=[pltpu.VMEM((STEPS_HERE, EX_HERE, P_SIZE), F32), dma((STEPS_HERE // 2,))],
        compiler_params=pltpu.CompilerParams(vmem_limit_bytes=16 * 1024 * 1024),
    )(rows, last, diag)


def solution(mesh):
    in_specs = (P("step", "ex", None), P("step"))
    out_specs = P("step", "ex", None)
    return jax.shard_map(
        per_device, mesh=mesh, in_specs=in_specs, out_specs=out_specs, check_vma=False
    )
```

```python
import functools
import math

import jax
import jax.numpy as jnp
from jax import lax
from jax.experimental import pallas as pl
from jax.experimental.pallas import tpu as pltpu
from jax.sharding import PartitionSpec as P

P_SIZE = 512
BATCH = 1024
NX, NY, NZ = 4, 4, 8
STEPS_HERE = 8
EX_HERE = 128
TILE = 128
ABOVE = [(a, b) for a in range(4) for b in range(a + 1, 4)]
PAIRS = [(0, 1), (2, 3)]
PACK = 16 + (len(ABOVE) + len(PAIRS)) * TILE
CUT = PACK // 4 // 16 * 16
PARTS = ((0, CUT), (CUT, CUT), (2 * CUT, CUT), (3 * CUT, PACK - 3 * CUT))
PIECE = 64
F32, BF16 = jnp.float32, jnp.bfloat16
MESH = pl.DeviceIdType.MESH


def dot_nn(a, b):
    return lax.dot_general(a, b, (((1,), (0,)), ((), ())), preferred_element_type=F32)


def dot_tn(a, b):
    return lax.dot_general(a, b, (((0,), (0,)), ((), ())), preferred_element_type=F32)


def two_parts(v):
    hi = v.astype(BF16)
    return hi, (v - hi.astype(F32)).astype(BF16)


def eye_mask(rows, columns, row0):
    r = lax.broadcasted_iota(jnp.int32, (rows, columns), 0) + row0
    return r == lax.broadcasted_iota(jnp.int32, (rows, columns), 1)


def times_rows(x_ref, diag, off_ref):
    x = x_ref[...]
    n = x.shape[0]
    y = dot_nn(jnp.concatenate(two_parts(x), axis=0), off_ref[...])
    x_ref[...] = x * diag + (y[:n] + y[n:])


def rows_plus_diag(x_ref, diag, off_ref, start):
    n = x_ref.shape[0]
    x_ref[...] = off_ref[pl.ds(start, n), :].astype(F32) + jnp.where(eye_mask(n, P_SIZE, start), diag, 0.0)


def rows_less_diag(x_ref, diag, off_ref, start):
    x = x_ref[...]
    off_ref[...] = (x - jnp.where(eye_mask(x.shape[0], P_SIZE, start), diag, 0.0)).astype(BF16)


def apply_part(x_ref, diag, off_ref, at, count):
    x = x_ref[pl.ds(at, count)].reshape(count * EX_HERE, P_SIZE)
    x = x * diag + dot_nn(x.astype(BF16), off_ref[...])
    x_ref[pl.ds(at, count)] = x.reshape(count, EX_HERE, P_SIZE)


def loop(first, last, run):
    def one(i, _):
        run(i)
        return 0

    lax.fori_loop(first, last, one, 0)


def choose(k, table):
    value = table[0]
    for i in range(1, len(table)):
        value = jnp.where(k == i, table[i], value)
    return value


def body(g_hbm, rate_hbm, out_ref, last_ref, last_diag, g_ref, rate_ref, gather, stage_r, stage_l, pack, maps, diags, v,
         few, mine, blocks, block_diags, mine_t, lines, line_diags,
         in_sem, g_send, g_recv, st_recv, p_send, p_recv,
         b_send, b_recv, bd_send, bd_recv, t_send, t_recv, td_send, td_recv):
    step, ex = lax.axis_index("step"), lax.axis_index("ex")
    y, z = step // NZ, step % NZ
    x, c = ex // 2, ex % 2
    xr, xl, xo = (x + 1) % NX, (x + 3) % NX, (x + 2) % NX
    sib = (step, x * 2 + 1 - c)
    right, left = (step, xr * 2 + c), (step, xl * 2 + c)
    z_next, z_prev = (y * NZ + (z + 1) % NZ, ex), (y * NZ + (z + NZ - 1) % NZ, ex)
    y_next, y_prev = (((y + 1) % NY) * NZ + z, ex), (((y + NY - 1) % NY) * NZ + z, ex)

    barrier = pltpu.get_barrier_semaphore()
    peers = [sib, right, left, (step, xr * 2 + 1 - c), (step, xl * 2 + 1 - c), z_next, z_prev, y_next, y_prev]
    for peer in peers:
        pl.semaphore_signal(barrier, inc=1, device_id=peer, device_id_type=MESH)
    pl.semaphore_wait(barrier, len(peers))

    def remote(src, dst, send, recv, device):
        return pltpu.make_async_remote_copy(
            src_ref=src, dst_ref=dst, send_sem=send, recv_sem=recv, device_id=device, device_id_type=MESH
        )

    started = []

    def go(copy):
        copy.start()
        started.append(copy)

    def all_sent(count):
        for copy in started[:count]:
            copy.wait_send()
        del started[:count]

    half = EX_HERE // 2

    def send_set(core):
        n = 1 + core * 6
        step_o, step_r, step_l = xo * 2 + core, xr * 2 + core, xl * 2 + core
        go(remote(g_hbm.at[step_o, pl.ds(0, half), :], stage_r.at[core], g_send.at[n], st_recv.at[core, 0], right))
        go(remote(g_hbm.at[step_o, pl.ds(half, half), :], stage_l.at[core], g_send.at[n + 1], st_recv.at[core, 1],
                  left))
        go(remote(g_hbm.at[step_r], gather.at[ex], g_send.at[n + 2], g_recv.at[ex, 0], (step, step_r)))
        go(remote(g_hbm.at[step_l], gather.at[ex], g_send.at[n + 3], g_recv.at[ex, 0], (step, step_l)))

    def forward_set(core):
        n = 1 + core * 6
        remote(stage_r.at[core], stage_r.at[core], g_send.at[0], st_recv.at[core, 0], sib).wait_recv()
        go(remote(stage_r.at[core], gather.at[xl * 2 + c, pl.ds(0, half), :], g_send.at[n + 4],
                  g_recv.at[xl * 2 + c, 0], (step, xr * 2 + core)))
        remote(stage_l.at[core], stage_l.at[core], g_send.at[0], st_recv.at[core, 1], sib).wait_recv()
        go(remote(stage_l.at[core], gather.at[xr * 2 + c, pl.ds(half, half), :], g_send.at[n + 5],
                  g_recv.at[xr * 2 + c, 1], (step, xl * 2 + core)))

    go(remote(g_hbm.at[x * 2 + 1 - c], gather.at[ex], g_send.at[0], g_recv.at[ex, 0], sib))
    send_set(0)
    own_in = pltpu.make_async_copy(g_hbm.at[ex], gather.at[ex], in_sem.at[0])
    all_in = pltpu.make_async_copy(g_hbm, g_ref, in_sem.at[1])
    rate_in = pltpu.make_async_copy(rate_hbm, rate_ref, in_sem.at[2])
    own_in.start()
    all_in.start()
    rate_in.start()
    forward_set(0)
    send_set(1)
    own_in.wait()
    rate_in.wait()

    def gram_of(chip, first):
        rows = gather[pl.ds(chip * 2, 2)].reshape(2 * EX_HERE, P_SIZE)
        if first:
            v[...] = dot_tn(rows, rows)
        else:
            v[...] += dot_tn(rows, rows)

    def arrived(source):
        remote(gather.at[source], gather.at[source], g_send.at[0], g_recv.at[source, 0], sib).wait_recv()

    def arrived_half(source, which):
        part = gather.at[source, pl.ds(which * half, half), :]
        remote(part, part, g_send.at[0], g_recv.at[source, which], sib).wait_recv()

    def gram_near():
        arrived(x * 2 + 1 - c)
        gram_of(x, True)

    def gram_far():
        for at in (xr, xl):
            for core in range(2):
                arrived(at * 2 + core)
            gram_of(at, False)
        for core in range(2):
            for which in range(2):
                arrived_half(xo * 2 + core, which)
        gram_of(xo, False)

    edge = (math.sqrt(BATCH) + math.sqrt(P_SIZE)) ** 2
    scale = rate_ref[ex] / edge
    own = pack.at[ex]
    row_at = lax.broadcasted_iota(jnp.int32, (TILE, TILE), 0)
    column_at = lax.broadcasted_iota(jnp.int32, (TILE, TILE), 1)
    on, upper, lower = row_at == column_at, row_at < column_at, row_at > column_at

    def pack_map():
        def map_tile(a, b):
            return v[pl.ds(a * TILE, TILE), pl.ds(b * TILE, TILE)] * (-scale)

        diag_parts = []
        for a in range(4):
            d = 1.0 + jnp.sum(jnp.where(on, map_tile(a, a), 0.0), axis=0, keepdims=True)
            d_hi, d_rest = d.astype(BF16).astype(F32), d - d.astype(BF16).astype(F32)
            d_mid = d_rest.astype(BF16).astype(F32)
            diag_parts.append((d_hi, d_mid, d_rest - d_mid))
        for n, (a, b) in enumerate(ABOVE):
            own[pl.ds(16 + n * TILE, TILE), :] = map_tile(a, b).astype(BF16)
        for n, (a, b) in enumerate(PAIRS):
            both = jnp.where(upper, map_tile(a, a), jnp.where(lower, map_tile(b, b), 0.0))
            own[pl.ds(16 + (len(ABOVE) + n) * TILE, TILE), :] = both.astype(BF16)
        rows = [diag_parts[a][part] for part in range(3) for a in range(4)]
        own[pl.ds(0, 16), :] = jnp.concatenate(rows + [jnp.zeros((4, TILE), F32)], axis=0).astype(BF16)

    def packed(slot, which):
        at, size = (0, PACK) if which == 4 else PARTS[which]
        return pack.at[slot, pl.ds(at, size), :]

    p_count = [0]

    def send_pack(slot, which, device):
        n = p_count[0]
        p_count[0] += 1
        go(remote(packed(slot, which), packed(slot, which), p_send.at[n], p_recv.at[slot, which], device))

    def got_pack(slot, which):
        remote(packed(slot, which), packed(slot, which), p_send.at[0], p_recv.at[slot, which], sib).wait_recv()

    def unpack(slot):
        parts = pack[slot, pl.ds(0, 16), :].astype(F32)
        diag = parts[0:4] + (parts[4:8] + parts[8:12])
        for a in range(4):
            diags[slot, :, pl.ds(a * TILE, TILE)] = diag[a:a + 1]

        def put(a, b, tile):
            maps[slot, pl.ds(a * TILE, TILE), pl.ds(b * TILE, TILE)] = tile

        for n, (a, b) in enumerate(ABOVE):
            tile = pack[slot, pl.ds(16 + n * TILE, TILE), :]
            put(a, b, tile)
            put(b, a, tile.T)
        for n, (a, b) in enumerate(PAIRS):
            tile = pack[slot, pl.ds(16 + (len(ABOVE) + n) * TILE, TILE), :].astype(F32)
            turned = tile.T
            put(a, a, jnp.where(upper, tile, turned).astype(BF16))
            put(b, b, jnp.where(lower, tile, turned).astype(BF16))

    first = []
    for which, device in ((0, left), (2, right), (1, left), (3, right), (2, left), (0, right), (3, left), (1, right),
                          (4, sib)):
        n = len(first)
        first.append(remote(packed(ex, which), packed(ex, which), p_send.at[n], p_recv.at[ex, which], device))
    p_count[0] = len(first)

    def send_first():
        for copy in first:
            copy.start()

    @pl.when(c == 0)
    def _():
        gram_near()
        gram_far()
        pack_map()

    @pl.when(c == 1)
    def _():
        gram_near()

    forward_set(1)

    @pl.when(c == 0)
    def _():
        send_first()

    @pl.when(c == 1)
    def _():
        gram_far()
        pack_map()
        send_first()

    started.extend(first)
    all_in.wait()
    from_right, from_left, across = xr * 2 + c, xl * 2 + c, xo * 2 + c
    unpack(ex)
    for s in range(STEPS_HERE):
        out_ref[s] = g_ref[s].astype(F32)

    def take(chip):
        got_pack(chip * 2 + 1 - c, 4)
        unpack(chip * 2 + 1 - c)

    @pl.when(c == 1)
    def _():
        take(x)

    for which in range(2):
        got_pack(from_right, which)
        send_pack(from_right, which, left)
        got_pack(from_left, 2 + which)
        send_pack(from_left, 2 + which, right)
    for which in range(2):
        got_pack(from_right, 2 + which)
        got_pack(from_left, which)
    send_pack(from_right, 4, sib)
    send_pack(from_left, 4, sib)
    unpack(from_right)
    unpack(from_left)

    @pl.when(c == 1)
    def _():
        take(xr)
        take(xl)

    for which in range(4):
        got_pack(across, which)
    send_pack(across, 4, sib)
    unpack(across)

    @pl.when(c == 0)
    def _():
        take(x)
        take(xr)
        take(xl)

    take(xo)

    quarters = (x % 2) * 2
    start = pl.multiple_of((c * 4 + quarters) * PIECE, 2 * PIECE)
    rows_plus_diag(few, diags[0], maps.at[0], start)
    for s in range(1, STEPS_HERE):
        times_rows(few, diags[s], maps.at[s])
    block_diag = diags[0]
    for s in range(1, STEPS_HERE):
        block_diag = block_diag * diags[s]
    block_diags[z] = block_diag
    rows_less_diag(few, block_diag, mine, start)
    blocks[z, pl.ds(start, 2 * PIECE), :] = mine[...]

    def single(j):
        apply_part(out_ref, diags[j * 2 + 1], maps.at[j * 2 + 1], j * 2, 1)

    def unit(u):
        s = choose(u, (2, 3, 4, 4, 5, 5, 6, 6, 6, 7, 7, 7))
        pair = choose(u, (0, 0, 0, 1, 0, 1, 0, 1, 2, 0, 1, 2))
        apply_part(out_ref, diags[s], maps.at[s], pair * 2, 2)

    def later(u):
        slot = z + 1 + u // 4
        apply_part(out_ref, block_diags[slot], blocks.at[slot], (u % 4) * 2, 2)

    units = 4 * (NZ - 1 - z)

    def later_units(first, last):
        loop(jnp.minimum(first, units), jnp.minimum(last, units), later)

    early = z < NZ // 2
    inner_done = jnp.where(early, 12, 5)

    def ring(own, buf, dbuf, n, pos, ahead, behind, send, recv, d_send, d_recv, own_too, before):
        a_at = jnp.where(x == 3, 1, 0)
        to_left = jnp.where(x == 1, 0, 1)
        base = c * 4 + quarters
        p_a, p_b = base + a_at, base + 1 - a_at
        turns = n // 2

        def rows(slot, at, count):
            return buf.at[slot, pl.ds(pl.multiple_of(at * PIECE, PIECE), count * PIECE), :]

        def pass_on(slot, at, count, kind, land, device, src=None):
            there = rows(slot, at, count)
            go(remote(there if src is None else src, there, send.at[slot, kind], recv.at[slot, land], device))

        def got(slot, at, count, land):
            there = rows(slot, at, count)
            remote(there, there, send.at[slot, 0], recv.at[slot, land], sib).wait_recv()

        def pass_diag(slot, kind, device):
            go(remote(dbuf.at[slot], dbuf.at[slot], d_send.at[slot, kind], d_recv.at[slot], device))

        def got_diag(slot):
            remote(dbuf.at[slot], dbuf.at[slot], d_send.at[slot, 0], d_recv.at[slot], sib).wait_recv()

        def part(src, at):
            return None if src is None else src.at[pl.ds(pl.multiple_of(at * PIECE, PIECE), PIECE), :]

        def left_copy(slot, src=None):
            there = rows(slot, base + to_left, 1)
            mine_there = part(src, to_left)
            return remote(there if src is None else mine_there, there, send.at[slot, 5],
                          recv.at[slot, 2 + to_left], left)

        def over_a(slot, src=None):
            pass_on(slot, p_a, 1, 4, 2 + a_at, right, part(src, a_at))
            copy = left_copy(slot, src)

            @pl.when(x % 2 == 1)
            def _():
                copy.start()

            started.append(copy)

        def over_b(slot, src=None):
            copy = left_copy(slot, src)

            @pl.when(x % 2 == 0)
            def _():
                copy.start()

        def to_sibling(slot, src=None):
            pass_on(slot, base, 2, 6, 4, sib, src)

        other = c * 4 + 2 - quarters

        def over_x(slot):
            got(slot, other, 1, 2)
            got(slot, other + 1, 1, 3)
            pass_on(slot, other, 2, 7, 5, sib)

        def got_all(slot):
            got(slot, (1 - c) * 4 + quarters, 2, 4)
            got(slot, (1 - c) * 4 + 2 - quarters, 2, 5)

        own_a, own_b = part(own, a_at), part(own, 1 - a_at)
        pass_on(pos, p_a, 1, 0, 0, ahead, own_a)
        pass_on(pos, p_b, 1, 3, 1, behind, own_b)
        pass_on(pos, p_b, 1, 1, 1, ahead, own_b)
        pass_on(pos, p_a, 1, 2, 0, behind, own_a)
        pass_diag(pos, 0, ahead)
        pass_diag(pos, 1, behind)
        if own_too:
            over_a(pos, own)
            over_b(pos, own)
            to_sibling(pos, own)

        waiting = [pos] if own_too else []
        for s in range(turns):
            last = s == turns - 1
            up, down = (pos + n - 1 - s) % n, (pos + 1 + s) % n
            before[s](got_all)
            got(up, p_a, 1, 0)
            if not last:
                pass_on(up, p_a, 1, 0, 0, ahead)
            over_a(up)
            got(down, p_b, 1, 1)
            if not last:
                pass_on(down, p_b, 1, 3, 1, behind)
            over_b(down)
            if last:
                to_sibling(up)
            else:
                got(up, p_b, 1, 1)
                if s < turns - 2:
                    pass_on(up, p_b, 1, 1, 1, ahead)
                over_b(up)
                got(down, p_a, 1, 0)
                if s < turns - 2:
                    pass_on(down, p_a, 1, 2, 0, behind)
                over_a(down)
                to_sibling(up)
                to_sibling(down)
            got_diag(up)
            if not last:
                pass_diag(up, 0, ahead)
                got_diag(down)
                if s < turns - 2:
                    pass_diag(down, 1, behind)
            for slot in waiting:
                over_x(slot)
            waiting = [up] if last else [up, down]
        before[turns](got_all)
        for slot in waiting:
            over_x(slot)

        return got_all

    before_ring = len(started)

    def first_fill(got_all):
        loop(0, STEPS_HERE // 2, single)
        loop(0, inner_done, unit)
        all_sent(before_ring)

    def block_fill(d):
        def run(got_all):
            got_all((z + d) % NZ)

            @pl.when(early)
            def _():
                loop(4 * d - 4, 4 * d, later)

        return run

    def last_fill(got_all):
        got_all((z + 3) % NZ)
        for d in (0, 5, 6, 7):
            got_all((z + d) % NZ)

        @pl.when(early)
        def _():
            loop(8, 12, later)

    got_all = ring(mine, blocks, block_diags, NZ, z, z_next, z_prev, b_send, b_recv, bd_send, bd_recv, True,
                   [first_fill, lambda _: None, block_fill(1), block_fill(2), last_fill])

    farthest = (z + NZ // 2) % NZ

    @pl.when(z >= NZ // 2)
    def _():
        got_all(farthest)

    rows_plus_diag(few, block_diags[0], blocks.at[0], start)
    for s in range(1, NZ // 2):
        times_rows(few, block_diags[s], blocks.at[s])

    @pl.when(early)
    def _():
        got_all(farthest)

    for s in range(NZ // 2, NZ):
        times_rows(few, block_diags[s], blocks.at[s])
    line_diag = block_diags[0]
    for s in range(1, NZ):
        line_diag = line_diag * block_diags[s]
    line_diags[y] = line_diag
    rows_less_diag(few, line_diag, mine_t, start)

    done = jnp.where(early, 12, 0)
    before_line = len(started)

    def line_fill(got_all):
        loop(inner_done, 12, unit)
        later_units(done, done + 8)
        all_sent(before_line)

    got_all = ring(mine_t, lines, line_diags, NY, y, y_next, y_prev, t_send, t_recv, td_send, td_recv, False,
                   [line_fill, lambda _: later_units(done + 8, done + 12), lambda _: None])
    later_units(done + 12, done + 28)

    for d in range(1, NY):
        slot = (y + d) % NY
        got_all(slot)

        @pl.when(y + d < NY - 1)
        def _():
            for at in (0, 4):
                apply_part(out_ref, line_diags[slot], lines.at[slot], at, 4)

    @pl.when(y < NY - 1)
    def _():
        last_ref[...] = lines[NY - 1]
        last_diag[...] = line_diags[NY - 1]

    @pl.when(y == NY - 1)
    def _():
        last_ref[...] = jnp.zeros_like(last_ref)
        last_diag[...] = jnp.ones_like(last_diag)

    all_sent(len(started))


def finish(x_ref, off_ref, diag_ref, out_hbm, held, sem):
    copies = []
    for i in range(STEPS_HERE // 2):
        x = x_ref[pl.ds(i * 2, 2)].reshape(2 * EX_HERE, P_SIZE)
        x = x * diag_ref[...] + dot_nn(x.astype(BF16), off_ref[...])
        held[pl.ds(i * 2, 2)] = x.reshape(2, EX_HERE, P_SIZE)
        copies.append(pltpu.make_async_copy(held.at[pl.ds(i * 2, 2)], out_hbm.at[pl.ds(i * 2, 2)], sem.at[i]))
        copies[-1].start()
    for copy in copies:
        copy.wait()


def per_device(gradients, step_rates):
    square = (P_SIZE, P_SIZE)
    dma = pltpu.SemaphoreType.DMA
    rows, last, diag = pl.pallas_call(
        body,
        out_shape=[jax.ShapeDtypeStruct(gradients.shape, F32), jax.ShapeDtypeStruct(square, BF16),
                   jax.ShapeDtypeStruct((1, P_SIZE), F32)],
        in_specs=[pl.BlockSpec(memory_space=pl.ANY)] * 2,
        out_specs=[pl.BlockSpec(memory_space=pltpu.VMEM)] * 3,
        scratch_shapes=[
            pltpu.VMEM((STEPS_HERE, EX_HERE, P_SIZE), BF16),
            pltpu.SMEM((STEPS_HERE,), F32),
            pltpu.VMEM((8, EX_HERE, P_SIZE), BF16),
            pltpu.VMEM((2, EX_HERE // 2, P_SIZE), BF16),
            pltpu.VMEM((2, EX_HERE // 2, P_SIZE), BF16),
            pltpu.VMEM((STEPS_HERE, PACK, TILE), BF16),
            pltpu.VMEM((STEPS_HERE,) + square, BF16),
            pltpu.VMEM((STEPS_HERE, 1, P_SIZE), F32),
            pltpu.VMEM(square, F32),
            pltpu.VMEM((2 * PIECE, P_SIZE), F32),
            pltpu.VMEM((2 * PIECE, P_SIZE), BF16),
            pltpu.VMEM((NZ,) + square, BF16),
            pltpu.VMEM((NZ, 1, P_SIZE), F32),
            pltpu.VMEM((2 * PIECE, P_SIZE), BF16),
            pltpu.VMEM((NY,) + square, BF16),
            pltpu.VMEM((NY, 1, P_SIZE), F32),
            dma((3,)),
            dma((13,)), dma((8, 2)), dma((2, 2)), dma((16,)), dma((8, 5)),
            dma((NZ, 8)), dma((NZ, 6)), dma((NZ, 2)), dma((NZ,)),
            dma((NY, 8)), dma((NY, 6)), dma((NY, 2)), dma((NY,)),
        ],
        compiler_params=pltpu.CompilerParams(
            collective_id=0, has_side_effects=True, vmem_limit_bytes=48 * 1024 * 1024
        ),
    )(pltpu.with_memory_space_constraint(gradients, pltpu.HBM),
      pltpu.with_memory_space_constraint(step_rates, pltpu.HBM))
    return pl.pallas_call(
        finish,
        out_shape=jax.ShapeDtypeStruct(gradients.shape, F32),
        in_specs=[pl.BlockSpec(memory_space=pltpu.VMEM)] * 3,
        out_specs=pl.BlockSpec(memory_space=pl.ANY),
        scratch_shapes=[pltpu.VMEM((STEPS_HERE, EX_HERE, P_SIZE), F32), dma((STEPS_HERE // 2,))],
        compiler_params=pltpu.CompilerParams(vmem_limit_bytes=16 * 1024 * 1024),
    )(rows, last, diag)


def solution(mesh):
    in_specs = (P("step", "ex", None), P("step"))
    out_specs = P("step", "ex", None)
    return jax.shard_map(
        per_device, mesh=mesh, in_specs=in_specs, out_specs=out_specs, check_vma=False
    )
```

```python
import functools
import math

import jax
import jax.numpy as jnp
from jax import lax
from jax.experimental import pallas as pl
from jax.experimental.pallas import tpu as pltpu
from jax.sharding import PartitionSpec as P

P_SIZE = 512
BATCH = 1024
NX, NY, NZ = 4, 4, 8
STEPS_HERE = 8
EX_HERE = 128
TILE = 128
ABOVE = [(a, b) for a in range(4) for b in range(a + 1, 4)]
PAIRS = [(0, 1), (2, 3)]
PACK = 16 + (len(ABOVE) + len(PAIRS)) * TILE
PARTS = ((0, 16 + 2 * TILE),) + tuple((16 + at * TILE, 2 * TILE) for at in (2, 4, 6))
PIECE = 64
F32, BF16 = jnp.float32, jnp.bfloat16
MESH = pl.DeviceIdType.MESH


def dot_nn(a, b):
    return lax.dot_general(a, b, (((1,), (0,)), ((), ())), preferred_element_type=F32)


def dot_tn(a, b):
    return lax.dot_general(a, b, (((0,), (0,)), ((), ())), preferred_element_type=F32)


def times_rows(x_ref, column, diag, off_ref, start):
    x = x_ref[...]
    here = off_ref[pl.ds(start, x.shape[0]), :].astype(F32)
    x_ref[...] = (x * diag + column * here) + dot_nn(x.astype(BF16), off_ref[...])


def running_diags(diag_ref, count, held, start):
    product = diag_ref[0]
    held[pl.ds(0, 1), :] = product
    for s in range(1, count):
        product = product * diag_ref[s]
        held[pl.ds(s, 1), :] = product
    rows = held[:, pl.ds(start, TILE)]
    columns = jnp.concatenate([rows, jnp.zeros((TILE - rows.shape[0], TILE), F32)], axis=0).T
    return product, [columns[:, s:s + 1] for s in range(count)]


def apply_part(x_ref, diag, off_ref, at, count):
    x = x_ref[pl.ds(at, count)].reshape(count * EX_HERE, P_SIZE)
    x = x * diag + dot_nn(x.astype(BF16), off_ref[...])
    x_ref[pl.ds(at, count)] = x.reshape(count, EX_HERE, P_SIZE)


def loop(first, last, run):
    def one(i, _):
        run(i)
        return 0

    lax.fori_loop(first, last, one, 0)


def choose(k, table):
    value = table[0]
    for i in range(1, len(table)):
        value = jnp.where(k == i, table[i], value)
    return value


def body(g_hbm, rate_hbm, out_ref, last_ref, last_diag, g_ref, rate_ref, gather, stage_r, stage_l, pack, maps, diags, v,
         few, held, mine, blocks, block_diags, mine_t, lines, line_diags,
         in_sem, g_send, g_recv, st_recv, p_send, p_recv,
         b_send, b_recv, bd_send, bd_recv, t_send, t_recv, td_send, td_recv):
    step, ex = lax.axis_index("step"), lax.axis_index("ex")
    y, z = step // NZ, step % NZ
    x, c = ex // 2, ex % 2
    xr, xl, xo = (x + 1) % NX, (x + 3) % NX, (x + 2) % NX
    sib = (step, x * 2 + 1 - c)
    right, left = (step, xr * 2 + c), (step, xl * 2 + c)
    z_next, z_prev = (y * NZ + (z + 1) % NZ, ex), (y * NZ + (z + NZ - 1) % NZ, ex)
    y_next, y_prev = (((y + 1) % NY) * NZ + z, ex), (((y + NY - 1) % NY) * NZ + z, ex)

    barrier = pltpu.get_barrier_semaphore()
    peers = [sib, right, left, (step, xr * 2 + 1 - c), (step, xl * 2 + 1 - c), z_next, z_prev, y_next, y_prev]
    for peer in peers:
        pl.semaphore_signal(barrier, inc=1, device_id=peer, device_id_type=MESH)
    pl.semaphore_wait(barrier, len(peers))

    def remote(src, dst, send, recv, device):
        return pltpu.make_async_remote_copy(
            src_ref=src, dst_ref=dst, send_sem=send, recv_sem=recv, device_id=device, device_id_type=MESH
        )

    started = []

    def go(copy):
        copy.start()
        started.append(copy)

    def all_sent(count):
        for copy in started[:count]:
            copy.wait_send()
        del started[:count]

    half = EX_HERE // 2

    def send_set(core):
        n = 1 + core * 6
        step_o, step_r, step_l = xo * 2 + core, xr * 2 + core, xl * 2 + core
        go(remote(g_hbm.at[step_o, pl.ds(0, half), :], stage_r.at[core], g_send.at[n], st_recv.at[core, 0], right))
        go(remote(g_hbm.at[step_o, pl.ds(half, half), :], stage_l.at[core], g_send.at[n + 1], st_recv.at[core, 1],
                  left))
        go(remote(g_hbm.at[step_r], gather.at[ex], g_send.at[n + 2], g_recv.at[ex, 0], (step, step_r)))
        go(remote(g_hbm.at[step_l], gather.at[ex], g_send.at[n + 3], g_recv.at[ex, 0], (step, step_l)))

    def forward_set(core):
        n = 1 + core * 6
        remote(stage_r.at[core], stage_r.at[core], g_send.at[0], st_recv.at[core, 0], sib).wait_recv()
        go(remote(stage_r.at[core], gather.at[xl * 2 + c, pl.ds(0, half), :], g_send.at[n + 4],
                  g_recv.at[xl * 2 + c, 0], (step, xr * 2 + core)))
        remote(stage_l.at[core], stage_l.at[core], g_send.at[0], st_recv.at[core, 1], sib).wait_recv()
        go(remote(stage_l.at[core], gather.at[xr * 2 + c, pl.ds(half, half), :], g_send.at[n + 5],
                  g_recv.at[xr * 2 + c, 1], (step, xl * 2 + core)))

    go(remote(g_hbm.at[x * 2 + 1 - c], gather.at[ex], g_send.at[0], g_recv.at[ex, 0], sib))
    send_set(0)
    own_in = pltpu.make_async_copy(g_hbm.at[ex], gather.at[ex], in_sem.at[0])
    all_in = pltpu.make_async_copy(g_hbm, g_ref, in_sem.at[1])
    rate_in = pltpu.make_async_copy(rate_hbm, rate_ref, in_sem.at[2])
    own_in.start()
    all_in.start()
    rate_in.start()
    forward_set(0)
    send_set(1)
    own_in.wait()
    rate_in.wait()

    def gram_of(chip, first):
        rows = gather[pl.ds(chip * 2, 2)].reshape(2 * EX_HERE, P_SIZE)
        mid = P_SIZE // 2
        upper, lower = dot_tn(rows[:, :mid], rows), dot_tn(rows[:, mid:], rows[:, mid:])
        if first:
            v[:mid, :] = upper
            v[mid:, mid:] = lower
        else:
            v[:mid, :] += upper
            v[mid:, mid:] += lower

    def arrived(source):
        remote(gather.at[source], gather.at[source], g_send.at[0], g_recv.at[source, 0], sib).wait_recv()

    def arrived_half(source, which):
        part = gather.at[source, pl.ds(which * half, half), :]
        remote(part, part, g_send.at[0], g_recv.at[source, which], sib).wait_recv()

    def gram_near():
        arrived(x * 2 + 1 - c)
        gram_of(x, True)

    def gram_far():
        for at in (xr, xl):
            for core in range(2):
                arrived(at * 2 + core)
            gram_of(at, False)
        for core in range(2):
            for which in range(2):
                arrived_half(xo * 2 + core, which)
        gram_of(xo, False)

    edge = (math.sqrt(BATCH) + math.sqrt(P_SIZE)) ** 2
    scale = rate_ref[ex] / edge
    own = pack.at[ex]
    row_at = lax.broadcasted_iota(jnp.int32, (TILE, TILE), 0)
    column_at = lax.broadcasted_iota(jnp.int32, (TILE, TILE), 1)
    on, upper, lower = row_at == column_at, row_at < column_at, row_at > column_at

    def map_tile(a, b):
        return v[pl.ds(a * TILE, TILE), pl.ds(b * TILE, TILE)] * (-scale)

    def pack_part(which):
        if which == 0:
            diag_parts = []
            for a in range(4):
                d = 1.0 + jnp.sum(jnp.where(on, map_tile(a, a), 0.0), axis=0, keepdims=True)
                d_hi, d_rest = d.astype(BF16).astype(F32), d - d.astype(BF16).astype(F32)
                d_mid = d_rest.astype(BF16).astype(F32)
                diag_parts.append((d_hi, d_mid, d_rest - d_mid))
            rows = [diag_parts[a][part] for part in range(3) for a in range(4)]
            own[pl.ds(0, 16), :] = jnp.concatenate(rows + [jnp.zeros((4, TILE), F32)], axis=0).astype(BF16)
        for n in (2 * which, 2 * which + 1):
            if n < len(ABOVE):
                tile = map_tile(*ABOVE[n])
            else:
                a, b = PAIRS[n - len(ABOVE)]
                tile = jnp.where(upper, map_tile(a, a), jnp.where(lower, map_tile(b, b), 0.0))
            own[pl.ds(16 + n * TILE, TILE), :] = tile.astype(BF16)

    def packed(slot, which):
        at, size = (0, PACK) if which == 4 else PARTS[which]
        return pack.at[slot, pl.ds(at, size), :]

    p_count = [0]

    def send_pack(slot, which, device):
        n = p_count[0]
        p_count[0] += 1
        go(remote(packed(slot, which), packed(slot, which), p_send.at[n], p_recv.at[slot, which], device))

    def got_pack(slot, which):
        remote(packed(slot, which), packed(slot, which), p_send.at[0], p_recv.at[slot, which], sib).wait_recv()

    def unpack_part(slot, which):
        def put(a, b, tile):
            maps[slot, pl.ds(a * TILE, TILE), pl.ds(b * TILE, TILE)] = tile

        if which == 0:
            parts = pack[slot, pl.ds(0, 16), :].astype(F32)
            diag = parts[0:4] + (parts[4:8] + parts[8:12])
            for a in range(4):
                diags[slot, :, pl.ds(a * TILE, TILE)] = diag[a:a + 1]
        for n in (2 * which, 2 * which + 1):
            tile = pack[slot, pl.ds(16 + n * TILE, TILE), :]
            if n < len(ABOVE):
                a, b = ABOVE[n]
                put(a, b, tile)
                put(b, a, tile.T)
            else:
                a, b = PAIRS[n - len(ABOVE)]
                tile = tile.astype(F32)
                turned = tile.T
                put(a, a, jnp.where(upper, tile, turned).astype(BF16))
                put(b, b, jnp.where(lower, tile, turned).astype(BF16))

    def unpack(slot):
        for which in range(4):
            unpack_part(slot, which)

    first = []
    for which, device in ((0, left), (2, right), (1, left), (3, right), (2, left), (0, right), (3, left), (1, right),
                          (4, sib)):
        n = len(first)
        first.append(remote(packed(ex, which), packed(ex, which), p_send.at[n], p_recv.at[ex, which], device))
    p_count[0] = len(first)

    def pack_all():
        for which in range(4):
            pack_part(which)

    def send_first():
        for copy in first:
            copy.start()

    @pl.when(c == 0)
    def _():
        gram_near()
        gram_far()
        pack_all()

    @pl.when(c == 1)
    def _():
        gram_near()

    forward_set(1)

    @pl.when(c == 0)
    def _():
        send_first()

    @pl.when(c == 1)
    def _():
        gram_far()
        for which, copy in zip((0, 2, 1, 3), first):
            pack_part(which)
            copy.start()
        for copy in first[4:]:
            copy.start()

    started.extend(first)
    all_in.wait()
    from_right, from_left, across = xr * 2 + c, xl * 2 + c, xo * 2 + c
    unpack(ex)
    for s in range(STEPS_HERE):
        out_ref[s] = g_ref[s].astype(F32)

    def take(chip):
        got_pack(chip * 2 + 1 - c, 4)
        unpack(chip * 2 + 1 - c)

    @pl.when(c == 1)
    def _():
        take(x)

    for which in range(2):
        got_pack(from_right, which)
        send_pack(from_right, which, left)
        got_pack(from_left, 2 + which)
        send_pack(from_left, 2 + which, right)
    for which in range(2):
        got_pack(from_right, 2 + which)
        got_pack(from_left, which)
    send_pack(from_right, 4, sib)
    send_pack(from_left, 4, sib)
    unpack(from_right)
    unpack(from_left)

    @pl.when(c == 1)
    def _():
        take(xr)
        take(xl)

    for which in range(4):
        got_pack(across, which)
        send_pack(across, which, sib)
    unpack(across)

    @pl.when(c == 0)
    def _():
        take(x)
        take(xr)
        take(xl)

    for which in range(4):
        got_pack(xo * 2 + 1 - c, which)
        unpack_part(xo * 2 + 1 - c, which)

    quarters = (x % 2) * 2
    start = pl.multiple_of((c * 4 + quarters) * PIECE, 2 * PIECE)
    block_diag, columns = running_diags(diags, STEPS_HERE, held, start)
    few[...] = maps[0, pl.ds(start, 2 * PIECE), :].astype(F32)
    for s in range(1, STEPS_HERE):
        times_rows(few, columns[s - 1], diags[s], maps.at[s], start)
    block_diags[z] = block_diag
    mine[...] = few[...].astype(BF16)
    blocks[z, pl.ds(start, 2 * PIECE), :] = mine[...]

    def single(j):
        apply_part(out_ref, diags[j * 2 + 1], maps.at[j * 2 + 1], j * 2, 1)

    def unit(u):
        s = choose(u, (2, 3, 4, 4, 5, 5, 6, 6, 6, 7, 7, 7))
        pair = choose(u, (0, 0, 0, 1, 0, 1, 0, 1, 2, 0, 1, 2))
        apply_part(out_ref, diags[s], maps.at[s], pair * 2, 2)

    def later(u):
        slot = z + 1 + u // 4
        apply_part(out_ref, block_diags[slot], blocks.at[slot], (u % 4) * 2, 2)

    units = 4 * (NZ - 1 - z)

    def later_units(first, last):
        loop(jnp.minimum(first, units), jnp.minimum(last, units), later)

    early = z < NZ // 2
    inner_done = jnp.where(early, 12, 5)

    def ring(own, buf, dbuf, n, pos, ahead, behind, send, recv, d_send, d_recv, own_too, before):
        a_at = jnp.where(x == 3, 1, 0)
        to_left = jnp.where(x == 1, 0, 1)
        base = c * 4 + quarters
        p_a, p_b = base + a_at, base + 1 - a_at
        turns = n // 2

        def rows(slot, at, count):
            return buf.at[slot, pl.ds(pl.multiple_of(at * PIECE, PIECE), count * PIECE), :]

        def pass_on(slot, at, count, kind, land, device, src=None):
            there = rows(slot, at, count)
            go(remote(there if src is None else src, there, send.at[slot, kind], recv.at[slot, land], device))

        def got(slot, at, count, land):
            there = rows(slot, at, count)
            remote(there, there, send.at[slot, 0], recv.at[slot, land], sib).wait_recv()

        def pass_diag(slot, kind, device):
            go(remote(dbuf.at[slot], dbuf.at[slot], d_send.at[slot, kind], d_recv.at[slot], device))

        def got_diag(slot):
            remote(dbuf.at[slot], dbuf.at[slot], d_send.at[slot, 0], d_recv.at[slot], sib).wait_recv()

        def part(src, at):
            return None if src is None else src.at[pl.ds(pl.multiple_of(at * PIECE, PIECE), PIECE), :]

        def left_copy(slot, src=None):
            there = rows(slot, base + to_left, 1)
            mine_there = part(src, to_left)
            return remote(there if src is None else mine_there, there, send.at[slot, 5],
                          recv.at[slot, 2 + to_left], left)

        def over_a(slot, src=None):
            pass_on(slot, p_a, 1, 4, 2 + a_at, right, part(src, a_at))
            copy = left_copy(slot, src)

            @pl.when(x % 2 == 1)
            def _():
                copy.start()

            started.append(copy)

        def over_b(slot, src=None):
            copy = left_copy(slot, src)

            @pl.when(x % 2 == 0)
            def _():
                copy.start()

        def to_sibling(slot, src=None):
            pass_on(slot, base, 2, 6, 4, sib, src)

        other = c * 4 + 2 - quarters

        def over_x(slot):
            got(slot, other, 1, 2)
            got(slot, other + 1, 1, 3)
            pass_on(slot, other, 2, 7, 5, sib)

        def got_all(slot):
            got(slot, (1 - c) * 4 + quarters, 2, 4)
            got(slot, (1 - c) * 4 + 2 - quarters, 2, 5)

        own_a, own_b = part(own, a_at), part(own, 1 - a_at)
        pass_on(pos, p_a, 1, 0, 0, ahead, own_a)
        pass_on(pos, p_b, 1, 3, 1, behind, own_b)
        pass_on(pos, p_b, 1, 1, 1, ahead, own_b)
        pass_on(pos, p_a, 1, 2, 0, behind, own_a)
        pass_diag(pos, 0, ahead)
        pass_diag(pos, 1, behind)
        if own_too:
            over_a(pos, own)
            over_b(pos, own)
            to_sibling(pos, own)

        waiting = [pos] if own_too else []
        for s in range(turns):
            last = s == turns - 1
            up, down = (pos + n - 1 - s) % n, (pos + 1 + s) % n
            before[s](got_all)
            got(up, p_a, 1, 0)
            if not last:
                pass_on(up, p_a, 1, 0, 0, ahead)
            over_a(up)
            got(down, p_b, 1, 1)
            if not last:
                pass_on(down, p_b, 1, 3, 1, behind)
            over_b(down)
            if last:
                to_sibling(up)
            else:
                got(up, p_b, 1, 1)
                if s < turns - 2:
                    pass_on(up, p_b, 1, 1, 1, ahead)
                over_b(up)
                got(down, p_a, 1, 0)
                if s < turns - 2:
                    pass_on(down, p_a, 1, 2, 0, behind)
                over_a(down)
                to_sibling(up)
                to_sibling(down)
            got_diag(up)
            if not last:
                pass_diag(up, 0, ahead)
                got_diag(down)
                if s < turns - 2:
                    pass_diag(down, 1, behind)
            for slot in waiting:
                over_x(slot)
            waiting = [up] if last else [up, down]
        before[turns](got_all)
        for slot in waiting:
            over_x(slot)

        return got_all

    before_ring = len(started)

    def first_fill(got_all):
        loop(0, STEPS_HERE // 2, single)
        loop(0, inner_done, unit)
        all_sent(before_ring)

    def block_fill(d):
        def run(got_all):
            got_all((z + d) % NZ)

            @pl.when(early)
            def _():
                loop(4 * d - 4, 4 * d, later)

        return run

    def last_fill(got_all):
        got_all((z + 3) % NZ)
        for d in (0, 5, 6, 7):
            got_all((z + d) % NZ)

        @pl.when(early)
        def _():
            loop(8, 12, later)

    got_all = ring(mine, blocks, block_diags, NZ, z, z_next, z_prev, b_send, b_recv, bd_send, bd_recv, True,
                   [first_fill, lambda _: None, block_fill(1), block_fill(2), last_fill])

    farthest = (z + NZ // 2) % NZ
    line_diag, columns = running_diags(block_diags, NZ, held, start)

    @pl.when(z >= NZ // 2)
    def _():
        got_all(farthest)

    few[...] = blocks[0, pl.ds(start, 2 * PIECE), :].astype(F32)
    for s in range(1, NZ // 2):
        times_rows(few, columns[s - 1], block_diags[s], blocks.at[s], start)

    @pl.when(early)
    def _():
        got_all(farthest)

    for s in range(NZ // 2, NZ):
        times_rows(few, columns[s - 1], block_diags[s], blocks.at[s], start)
    line_diags[y] = line_diag
    mine_t[...] = few[...].astype(BF16)

    done = jnp.where(early, 12, 0)
    before_line = len(started)

    def line_fill(got_all):
        loop(inner_done, 12, unit)
        later_units(done, done + 8)
        all_sent(before_line)

    got_all = ring(mine_t, lines, line_diags, NY, y, y_next, y_prev, t_send, t_recv, td_send, td_recv, False,
                   [line_fill, lambda _: later_units(done + 8, done + 12), lambda _: None])
    later_units(done + 12, done + 28)

    for d in range(1, NY):
        slot = (y + d) % NY
        got_all(slot)

        @pl.when(y + d < NY - 1)
        def _():
            for at in (0, 4):
                apply_part(out_ref, line_diags[slot], lines.at[slot], at, 4)

    @pl.when(y < NY - 1)
    def _():
        last_ref[...] = lines[NY - 1]
        last_diag[...] = line_diags[NY - 1]

    @pl.when(y == NY - 1)
    def _():
        last_ref[...] = jnp.zeros_like(last_ref)
        last_diag[...] = jnp.ones_like(last_diag)

    all_sent(len(started))


def finish(x_ref, off_ref, diag_ref, out_hbm, held, sem):
    copies = []
    for i in range(STEPS_HERE // 2):
        x = x_ref[pl.ds(i * 2, 2)].reshape(2 * EX_HERE, P_SIZE)
        x = x * diag_ref[...] + dot_nn(x.astype(BF16), off_ref[...])
        held[pl.ds(i * 2, 2)] = x.reshape(2, EX_HERE, P_SIZE)
        copies.append(pltpu.make_async_copy(held.at[pl.ds(i * 2, 2)], out_hbm.at[pl.ds(i * 2, 2)], sem.at[i]))
        copies[-1].start()
    for copy in copies:
        copy.wait()


def per_device(gradients, step_rates):
    square = (P_SIZE, P_SIZE)
    dma = pltpu.SemaphoreType.DMA
    rows, last, diag = pl.pallas_call(
        body,
        out_shape=[jax.ShapeDtypeStruct(gradients.shape, F32), jax.ShapeDtypeStruct(square, BF16),
                   jax.ShapeDtypeStruct((1, P_SIZE), F32)],
        in_specs=[pl.BlockSpec(memory_space=pl.ANY)] * 2,
        out_specs=[pl.BlockSpec(memory_space=pltpu.VMEM)] * 3,
        scratch_shapes=[
            pltpu.VMEM((STEPS_HERE, EX_HERE, P_SIZE), BF16),
            pltpu.SMEM((STEPS_HERE,), F32),
            pltpu.VMEM((8, EX_HERE, P_SIZE), BF16),
            pltpu.VMEM((2, EX_HERE // 2, P_SIZE), BF16),
            pltpu.VMEM((2, EX_HERE // 2, P_SIZE), BF16),
            pltpu.VMEM((STEPS_HERE, PACK, TILE), BF16),
            pltpu.VMEM((STEPS_HERE,) + square, BF16),
            pltpu.VMEM((STEPS_HERE, 1, P_SIZE), F32),
            pltpu.VMEM(square, F32),
            pltpu.VMEM((2 * PIECE, P_SIZE), F32),
            pltpu.VMEM((8, P_SIZE), F32),
            pltpu.VMEM((2 * PIECE, P_SIZE), BF16),
            pltpu.VMEM((NZ,) + square, BF16),
            pltpu.VMEM((NZ, 1, P_SIZE), F32),
            pltpu.VMEM((2 * PIECE, P_SIZE), BF16),
            pltpu.VMEM((NY,) + square, BF16),
            pltpu.VMEM((NY, 1, P_SIZE), F32),
            dma((3,)),
            dma((13,)), dma((8, 2)), dma((2, 2)), dma((19,)), dma((8, 5)),
            dma((NZ, 8)), dma((NZ, 6)), dma((NZ, 2)), dma((NZ,)),
            dma((NY, 8)), dma((NY, 6)), dma((NY, 2)), dma((NY,)),
        ],
        compiler_params=pltpu.CompilerParams(
            collective_id=0, has_side_effects=True, vmem_limit_bytes=48 * 1024 * 1024
        ),
    )(pltpu.with_memory_space_constraint(gradients, pltpu.HBM),
      pltpu.with_memory_space_constraint(step_rates, pltpu.HBM))
    return pl.pallas_call(
        finish,
        out_shape=jax.ShapeDtypeStruct(gradients.shape, F32),
        in_specs=[pl.BlockSpec(memory_space=pltpu.VMEM)] * 3,
        out_specs=pl.BlockSpec(memory_space=pl.ANY),
        scratch_shapes=[pltpu.VMEM((STEPS_HERE, EX_HERE, P_SIZE), F32), dma((STEPS_HERE // 2,))],
        compiler_params=pltpu.CompilerParams(vmem_limit_bytes=16 * 1024 * 1024),
    )(rows, last, diag)


def solution(mesh):
    in_specs = (P("step", "ex", None), P("step"))
    out_specs = P("step", "ex", None)
    return jax.shard_map(
        per_device, mesh=mesh, in_specs=in_specs, out_specs=out_specs, check_vma=False
    )
```

```python
import functools
import math

import jax
import jax.numpy as jnp
from jax import lax
from jax.experimental import pallas as pl
from jax.experimental.pallas import tpu as pltpu
from jax.sharding import PartitionSpec as P

P_SIZE = 512
BATCH = 1024
NX, NY, NZ = 4, 4, 8
STEPS_HERE = 8
EX_HERE = 128
TILE = 128
ABOVE = [(a, b) for a in range(4) for b in range(a + 1, 4)]
PAIRS = [(0, 1), (2, 3)]
PACK = 16 + (len(ABOVE) + len(PAIRS)) * TILE
PARTS = ((0, 16 + 2 * TILE),) + tuple((16 + at * TILE, 2 * TILE) for at in (2, 4, 6))
PIECE = 64
F32, BF16 = jnp.float32, jnp.bfloat16
MESH = pl.DeviceIdType.MESH


def dot_nn(a, b):
    return lax.dot_general(a, b, (((1,), (0,)), ((), ())), preferred_element_type=F32)


def dot_tn(a, b):
    return lax.dot_general(a, b, (((0,), (0,)), ((), ())), preferred_element_type=F32)


def times_rows(x_ref, column, diag, off_ref, start):
    x = x_ref[...]
    here = off_ref[pl.ds(start, x.shape[0]), :].astype(F32)
    x_ref[...] = (x * diag + column * here) + dot_nn(x.astype(BF16), off_ref[...])


def running_diags(diag_ref, count, held, start):
    product = diag_ref[0]
    held[pl.ds(0, 1), :] = product
    for s in range(1, count):
        product = product * diag_ref[s]
        held[pl.ds(s, 1), :] = product
    rows = held[:, pl.ds(start, TILE)]
    columns = jnp.concatenate([rows, jnp.zeros((TILE - rows.shape[0], TILE), F32)], axis=0).T
    return product, [columns[:, s:s + 1] for s in range(count)]


def apply_part(x_ref, diag, off_ref, at, count):
    x = x_ref[pl.ds(at, count)].reshape(count * EX_HERE, P_SIZE)
    x = x * diag + dot_nn(x.astype(BF16), off_ref[...])
    x_ref[pl.ds(at, count)] = x.reshape(count, EX_HERE, P_SIZE)


def loop(first, last, run):
    def one(i, _):
        run(i)
        return 0

    lax.fori_loop(first, last, one, 0)


def choose(k, table):
    value = table[0]
    for i in range(1, len(table)):
        value = jnp.where(k == i, table[i], value)
    return value


def body(g_hbm, rate_hbm, out_ref, last_ref, last_diag, g_ref, rate_ref, gather, stage_r, stage_l, pack, maps, diags, v,
         few, held, mine, blocks, block_diags, mine_t, lines, line_diags,
         in_sem, g_send, g_recv, st_recv, p_send, p_recv,
         b_send, b_recv, bd_send, bd_recv, t_send, t_recv, td_send, td_recv):
    step, ex = lax.axis_index("step"), lax.axis_index("ex")
    y, z = step // NZ, step % NZ
    x, c = ex // 2, ex % 2
    xr, xl, xo = (x + 1) % NX, (x + 3) % NX, (x + 2) % NX
    sib = (step, x * 2 + 1 - c)
    right, left = (step, xr * 2 + c), (step, xl * 2 + c)
    z_next, z_prev = (y * NZ + (z + 1) % NZ, ex), (y * NZ + (z + NZ - 1) % NZ, ex)
    y_next, y_prev = (((y + 1) % NY) * NZ + z, ex), (((y + NY - 1) % NY) * NZ + z, ex)

    barrier = pltpu.get_barrier_semaphore()
    peers = [sib, right, left, (step, xr * 2 + 1 - c), (step, xl * 2 + 1 - c), z_next, z_prev, y_next, y_prev]
    for peer in peers:
        pl.semaphore_signal(barrier, inc=1, device_id=peer, device_id_type=MESH)
    pl.semaphore_wait(barrier, len(peers))

    def remote(src, dst, send, recv, device):
        return pltpu.make_async_remote_copy(
            src_ref=src, dst_ref=dst, send_sem=send, recv_sem=recv, device_id=device, device_id_type=MESH
        )

    started = []

    def go(copy):
        copy.start()
        started.append(copy)

    def all_sent(count):
        for copy in started[:count]:
            copy.wait_send()
        del started[:count]

    half = EX_HERE // 2

    def send_set(core):
        n = 1 + core * 6
        step_o, step_r, step_l = xo * 2 + core, xr * 2 + core, xl * 2 + core
        go(remote(g_hbm.at[step_o, pl.ds(0, half), :], stage_r.at[core], g_send.at[n], st_recv.at[core, 0], right))
        go(remote(g_hbm.at[step_o, pl.ds(half, half), :], stage_l.at[core], g_send.at[n + 1], st_recv.at[core, 1],
                  left))
        go(remote(g_hbm.at[step_r], gather.at[ex], g_send.at[n + 2], g_recv.at[ex, 0], (step, step_r)))
        go(remote(g_hbm.at[step_l], gather.at[ex], g_send.at[n + 3], g_recv.at[ex, 0], (step, step_l)))

    def forward_set(core):
        n = 1 + core * 6
        remote(stage_r.at[core], stage_r.at[core], g_send.at[0], st_recv.at[core, 0], sib).wait_recv()
        go(remote(stage_r.at[core], gather.at[xl * 2 + c, pl.ds(0, half), :], g_send.at[n + 4],
                  g_recv.at[xl * 2 + c, 0], (step, xr * 2 + core)))
        remote(stage_l.at[core], stage_l.at[core], g_send.at[0], st_recv.at[core, 1], sib).wait_recv()
        go(remote(stage_l.at[core], gather.at[xr * 2 + c, pl.ds(half, half), :], g_send.at[n + 5],
                  g_recv.at[xr * 2 + c, 1], (step, xl * 2 + core)))

    go(remote(g_hbm.at[x * 2 + 1 - c], gather.at[ex], g_send.at[0], g_recv.at[ex, 0], sib))
    send_set(0)
    own_in = pltpu.make_async_copy(g_hbm.at[ex], gather.at[ex], in_sem.at[0])
    all_in = pltpu.make_async_copy(g_hbm, g_ref, in_sem.at[1])
    rate_in = pltpu.make_async_copy(rate_hbm, rate_ref, in_sem.at[2])
    own_in.start()
    all_in.start()
    rate_in.start()
    forward_set(0)
    send_set(1)
    own_in.wait()
    rate_in.wait()

    def gram_of(chip, first):
        rows = gather[pl.ds(chip * 2, 2)].reshape(2 * EX_HERE, P_SIZE)
        mid = P_SIZE // 2
        upper, lower = dot_tn(rows[:, :mid], rows), dot_tn(rows[:, mid:], rows[:, mid:])
        if first:
            v[:mid, :] = upper
            v[mid:, mid:] = lower
        else:
            v[:mid, :] += upper
            v[mid:, mid:] += lower

    def arrived(source):
        remote(gather.at[source], gather.at[source], g_send.at[0], g_recv.at[source, 0], sib).wait_recv()

    def arrived_half(source, which):
        part = gather.at[source, pl.ds(which * half, half), :]
        remote(part, part, g_send.at[0], g_recv.at[source, which], sib).wait_recv()

    def gram_near():
        arrived(x * 2 + 1 - c)
        gram_of(x, True)

    def gram_far():
        for at in (xr, xl):
            for core in range(2):
                arrived(at * 2 + core)
            gram_of(at, False)
        for core in range(2):
            for which in range(2):
                arrived_half(xo * 2 + core, which)
        gram_of(xo, False)

    edge = (math.sqrt(BATCH) + math.sqrt(P_SIZE)) ** 2
    scale = rate_ref[ex] / edge
    own = pack.at[ex]
    row_at = lax.broadcasted_iota(jnp.int32, (TILE, TILE), 0)
    column_at = lax.broadcasted_iota(jnp.int32, (TILE, TILE), 1)
    on, upper, lower = row_at == column_at, row_at < column_at, row_at > column_at

    def map_tile(a, b):
        return v[pl.ds(a * TILE, TILE), pl.ds(b * TILE, TILE)] * (-scale)

    def pack_part(which):
        if which == 0:
            diag_parts = []
            for a in range(4):
                d = 1.0 + jnp.sum(jnp.where(on, map_tile(a, a), 0.0), axis=0, keepdims=True)
                d_hi, d_rest = d.astype(BF16).astype(F32), d - d.astype(BF16).astype(F32)
                d_mid = d_rest.astype(BF16).astype(F32)
                diag_parts.append((d_hi, d_mid, d_rest - d_mid))
            rows = [diag_parts[a][part] for part in range(3) for a in range(4)]
            own[pl.ds(0, 16), :] = jnp.concatenate(rows + [jnp.zeros((4, TILE), F32)], axis=0).astype(BF16)
        for n in (2 * which, 2 * which + 1):
            if n < len(ABOVE):
                tile = map_tile(*ABOVE[n])
            else:
                a, b = PAIRS[n - len(ABOVE)]
                tile = jnp.where(upper, map_tile(a, a), jnp.where(lower, map_tile(b, b), 0.0))
            own[pl.ds(16 + n * TILE, TILE), :] = tile.astype(BF16)

    def packed(slot, which):
        at, size = (0, PACK) if which == 4 else PARTS[which]
        return pack.at[slot, pl.ds(at, size), :]

    p_count = [0]

    def send_pack(slot, which, device):
        n = p_count[0]
        p_count[0] += 1
        go(remote(packed(slot, which), packed(slot, which), p_send.at[n], p_recv.at[slot, which], device))

    def got_pack(slot, which):
        remote(packed(slot, which), packed(slot, which), p_send.at[0], p_recv.at[slot, which], sib).wait_recv()

    def unpack_part(slot, which):
        def put(a, b, tile):
            maps[slot, pl.ds(a * TILE, TILE), pl.ds(b * TILE, TILE)] = tile

        if which == 0:
            parts = pack[slot, pl.ds(0, 16), :].astype(F32)
            diag = parts[0:4] + (parts[4:8] + parts[8:12])
            for a in range(4):
                diags[slot, :, pl.ds(a * TILE, TILE)] = diag[a:a + 1]
        for n in (2 * which, 2 * which + 1):
            tile = pack[slot, pl.ds(16 + n * TILE, TILE), :]
            if n < len(ABOVE):
                a, b = ABOVE[n]
                put(a, b, tile)
                put(b, a, tile.T)
            else:
                a, b = PAIRS[n - len(ABOVE)]
                tile = tile.astype(F32)
                turned = tile.T
                put(a, a, jnp.where(upper, tile, turned).astype(BF16))
                put(b, b, jnp.where(lower, tile, turned).astype(BF16))

    def unpack(slot):
        for which in range(4):
            unpack_part(slot, which)

    first = []
    for which, device in ((0, left), (2, right), (1, left), (3, right), (2, left), (0, right), (3, left), (1, right),
                          (4, sib)):
        n = len(first)
        first.append(remote(packed(ex, which), packed(ex, which), p_send.at[n], p_recv.at[ex, which], device))
    p_count[0] = len(first)

    def pack_all():
        for which in range(4):
            pack_part(which)

    def send_first():
        for copy in first:
            copy.start()

    @pl.when(c == 0)
    def _():
        gram_near()
        gram_far()
        pack_all()

    @pl.when(c == 1)
    def _():
        gram_near()

    forward_set(1)

    @pl.when(c == 0)
    def _():
        send_first()

    @pl.when(c == 1)
    def _():
        gram_far()
        for which, copy in zip((0, 2, 1, 3), first):
            pack_part(which)
            copy.start()
        for copy in first[4:]:
            copy.start()

    started.extend(first)
    all_in.wait()
    from_right, from_left, across = xr * 2 + c, xl * 2 + c, xo * 2 + c
    unpack(ex)
    for s in range(STEPS_HERE):
        out_ref[s] = g_ref[s].astype(F32)

    def take(chip):
        got_pack(chip * 2 + 1 - c, 4)
        unpack(chip * 2 + 1 - c)

    @pl.when(c == 1)
    def _():
        take(x)

    for which in range(2):
        got_pack(from_right, which)
        send_pack(from_right, which, left)
        got_pack(from_left, 2 + which)
        send_pack(from_left, 2 + which, right)
    for which in range(2):
        got_pack(from_right, 2 + which)
        got_pack(from_left, which)
    send_pack(from_right, 4, sib)
    send_pack(from_left, 4, sib)
    unpack(from_right)
    unpack(from_left)

    @pl.when(c == 1)
    def _():
        take(xr)
        take(xl)

    for which in range(4):
        got_pack(across, which)
        send_pack(across, which, sib)
    unpack(across)

    @pl.when(c == 0)
    def _():
        take(x)
        take(xr)
        take(xl)

    for which in range(4):
        got_pack(xo * 2 + 1 - c, which)
        unpack_part(xo * 2 + 1 - c, which)

    quarters = (x % 2) * 2
    start = pl.multiple_of((c * 4 + quarters) * PIECE, 2 * PIECE)
    block_diag, columns = running_diags(diags, STEPS_HERE, held, start)
    few[...] = maps[0, pl.ds(start, 2 * PIECE), :].astype(F32)
    for s in range(1, STEPS_HERE):
        times_rows(few, columns[s - 1], diags[s], maps.at[s], start)
    block_diags[z] = block_diag
    mine[...] = few[...].astype(BF16)
    blocks[z, pl.ds(start, 2 * PIECE), :] = mine[...]

    def single(j):
        apply_part(out_ref, diags[j * 2 + 1], maps.at[j * 2 + 1], j * 2, 1)

    def unit(u):
        s = choose(u, (2, 3, 4, 4, 5, 5, 6, 6, 6, 7, 7, 7))
        pair = choose(u, (0, 0, 0, 1, 0, 1, 0, 1, 2, 0, 1, 2))
        apply_part(out_ref, diags[s], maps.at[s], pair * 2, 2)

    def later(u):
        slot = z + 1 + u // 4
        apply_part(out_ref, block_diags[slot], blocks.at[slot], (u % 4) * 2, 2)

    units = 4 * (NZ - 1 - z)

    def later_units(first, last):
        loop(jnp.minimum(first, units), jnp.minimum(last, units), later)

    early = z < NZ // 2
    inner_done = jnp.where(early, 12, 5)

    def ring(own, buf, dbuf, n, pos, ahead, behind, send, recv, d_send, d_recv, own_too, before):
        a_at = jnp.where(x == 3, 1, 0)
        to_left = jnp.where(x == 1, 0, 1)
        base = c * 4 + quarters
        p_a, p_b = base + a_at, base + 1 - a_at
        turns = n // 2

        def rows(slot, at, count):
            return buf.at[slot, pl.ds(pl.multiple_of(at * PIECE, PIECE), count * PIECE), :]

        def pass_on(slot, at, count, kind, land, device, src=None):
            there = rows(slot, at, count)
            go(remote(there if src is None else src, there, send.at[slot, kind], recv.at[slot, land], device))

        def got(slot, at, count, land):
            there = rows(slot, at, count)
            remote(there, there, send.at[slot, 0], recv.at[slot, land], sib).wait_recv()

        def pass_diag(slot, kind, device):
            go(remote(dbuf.at[slot], dbuf.at[slot], d_send.at[slot, kind], d_recv.at[slot], device))

        def got_diag(slot):
            remote(dbuf.at[slot], dbuf.at[slot], d_send.at[slot, 0], d_recv.at[slot], sib).wait_recv()

        def part(src, at):
            return None if src is None else src.at[pl.ds(pl.multiple_of(at * PIECE, PIECE), PIECE), :]

        def left_copy(slot, src=None):
            there = rows(slot, base + to_left, 1)
            mine_there = part(src, to_left)
            return remote(there if src is None else mine_there, there, send.at[slot, 5],
                          recv.at[slot, 2 + to_left], left)

        def over_a(slot, src=None):
            pass_on(slot, p_a, 1, 4, 2 + a_at, right, part(src, a_at))
            copy = left_copy(slot, src)

            @pl.when(x % 2 == 1)
            def _():
                copy.start()

            started.append(copy)

        def over_b(slot, src=None):
            copy = left_copy(slot, src)

            @pl.when(x % 2 == 0)
            def _():
                copy.start()

        def to_sibling(slot, src=None):
            pass_on(slot, base, 2, 6, 4, sib, src)

        other = c * 4 + 2 - quarters

        def over_x(slot):
            got(slot, other, 1, 2)
            got(slot, other + 1, 1, 3)
            pass_on(slot, other, 2, 7, 5, sib)

        def got_all(slot):
            got(slot, (1 - c) * 4 + quarters, 2, 4)
            got(slot, (1 - c) * 4 + 2 - quarters, 2, 5)

        own_a, own_b = part(own, a_at), part(own, 1 - a_at)
        pass_on(pos, p_a, 1, 0, 0, ahead, own_a)
        pass_on(pos, p_b, 1, 3, 1, behind, own_b)
        pass_on(pos, p_b, 1, 1, 1, ahead, own_b)
        pass_on(pos, p_a, 1, 2, 0, behind, own_a)
        pass_diag(pos, 0, ahead)
        pass_diag(pos, 1, behind)
        if own_too:
            over_a(pos, own)
            over_b(pos, own)
            to_sibling(pos, own)

        waiting = [pos] if own_too else []
        for s in range(turns):
            last = s == turns - 1
            up, down = (pos + n - 1 - s) % n, (pos + 1 + s) % n
            before[s](got_all)
            got(up, p_a, 1, 0)
            if not last:
                pass_on(up, p_a, 1, 0, 0, ahead)
            over_a(up)
            got(down, p_b, 1, 1)
            if not last:
                pass_on(down, p_b, 1, 3, 1, behind)
            over_b(down)
            if last:
                to_sibling(up)
            else:
                got(up, p_b, 1, 1)
                if s < turns - 2:
                    pass_on(up, p_b, 1, 1, 1, ahead)
                over_b(up)
                got(down, p_a, 1, 0)
                if s < turns - 2:
                    pass_on(down, p_a, 1, 2, 0, behind)
                over_a(down)
                to_sibling(up)
                to_sibling(down)
            got_diag(up)
            if not last:
                pass_diag(up, 0, ahead)
                got_diag(down)
                if s < turns - 2:
                    pass_diag(down, 1, behind)
            for slot in waiting:
                over_x(slot)
            waiting = [up] if last else [up, down]
        before[turns](got_all)
        for slot in waiting:
            over_x(slot)

        return got_all

    before_ring = len(started)

    def first_fill(got_all):
        loop(0, STEPS_HERE // 2, single)
        loop(0, inner_done, unit)

    def block_fill(got_all):
        for d in (1, 2):
            got_all((z + d) % NZ)

            @pl.when(early)
            def _():
                loop(4 * d - 4, 4 * d, later)

    def last_fill(got_all):
        all_sent(before_ring)
        got_all((z + 3) % NZ)
        for d in (0, 5, 6, 7):
            got_all((z + d) % NZ)

        @pl.when(early)
        def _():
            loop(8, 12, later)

    got_all = ring(mine, blocks, block_diags, NZ, z, z_next, z_prev, b_send, b_recv, bd_send, bd_recv, True,
                   [first_fill, lambda _: None, lambda _: None, block_fill, last_fill])

    farthest = (z + NZ // 2) % NZ
    line_diag, columns = running_diags(block_diags, NZ, held, start)

    @pl.when(z >= NZ // 2)
    def _():
        got_all(farthest)

    few[...] = blocks[0, pl.ds(start, 2 * PIECE), :].astype(F32)
    for s in range(1, NZ // 2):
        times_rows(few, columns[s - 1], block_diags[s], blocks.at[s], start)

    @pl.when(early)
    def _():
        got_all(farthest)

    for s in range(NZ // 2, NZ):
        times_rows(few, columns[s - 1], block_diags[s], blocks.at[s], start)
    line_diags[y] = line_diag
    mine_t[...] = few[...].astype(BF16)

    done = jnp.where(early, 12, 0)
    before_line = len(started)

    def line_fill(got_all):
        loop(inner_done, 12, unit)
        later_units(done, done + 8)

    got_all = ring(mine_t, lines, line_diags, NY, y, y_next, y_prev, t_send, t_recv, td_send, td_recv, False,
                   [line_fill, lambda _: later_units(done + 8, done + 12), lambda _: all_sent(before_line)])
    later_units(done + 12, done + 28)

    for d in range(1, NY):
        slot = (y + d) % NY
        got_all(slot)

        @pl.when(y + d < NY - 1)
        def _():
            for at in (0, 4):
                apply_part(out_ref, line_diags[slot], lines.at[slot], at, 4)

    @pl.when(y < NY - 1)
    def _():
        last_ref[...] = lines[NY - 1]
        last_diag[...] = line_diags[NY - 1]

    @pl.when(y == NY - 1)
    def _():
        last_ref[...] = jnp.zeros_like(last_ref)
        last_diag[...] = jnp.ones_like(last_diag)

    all_sent(len(started))


def finish(x_ref, off_ref, diag_ref, out_hbm, held, sem):
    copies = []
    for i in range(STEPS_HERE // 2):
        x = x_ref[pl.ds(i * 2, 2)].reshape(2 * EX_HERE, P_SIZE)
        x = x * diag_ref[...] + dot_nn(x.astype(BF16), off_ref[...])
        held[pl.ds(i * 2, 2)] = x.reshape(2, EX_HERE, P_SIZE)
        copies.append(pltpu.make_async_copy(held.at[pl.ds(i * 2, 2)], out_hbm.at[pl.ds(i * 2, 2)], sem.at[i]))
        copies[-1].start()
    for copy in copies:
        copy.wait()


def per_device(gradients, step_rates):
    square = (P_SIZE, P_SIZE)
    dma = pltpu.SemaphoreType.DMA
    rows, last, diag = pl.pallas_call(
        body,
        out_shape=[jax.ShapeDtypeStruct(gradients.shape, F32), jax.ShapeDtypeStruct(square, BF16),
                   jax.ShapeDtypeStruct((1, P_SIZE), F32)],
        in_specs=[pl.BlockSpec(memory_space=pl.ANY)] * 2,
        out_specs=[pl.BlockSpec(memory_space=pltpu.VMEM)] * 3,
        scratch_shapes=[
            pltpu.VMEM((STEPS_HERE, EX_HERE, P_SIZE), BF16),
            pltpu.SMEM((STEPS_HERE,), F32),
            pltpu.VMEM((8, EX_HERE, P_SIZE), BF16),
            pltpu.VMEM((2, EX_HERE // 2, P_SIZE), BF16),
            pltpu.VMEM((2, EX_HERE // 2, P_SIZE), BF16),
            pltpu.VMEM((STEPS_HERE, PACK, TILE), BF16),
            pltpu.VMEM((STEPS_HERE,) + square, BF16),
            pltpu.VMEM((STEPS_HERE, 1, P_SIZE), F32),
            pltpu.VMEM(square, F32),
            pltpu.VMEM((2 * PIECE, P_SIZE), F32),
            pltpu.VMEM((8, P_SIZE), F32),
            pltpu.VMEM((2 * PIECE, P_SIZE), BF16),
            pltpu.VMEM((NZ,) + square, BF16),
            pltpu.VMEM((NZ, 1, P_SIZE), F32),
            pltpu.VMEM((2 * PIECE, P_SIZE), BF16),
            pltpu.VMEM((NY,) + square, BF16),
            pltpu.VMEM((NY, 1, P_SIZE), F32),
            dma((3,)),
            dma((13,)), dma((8, 2)), dma((2, 2)), dma((19,)), dma((8, 5)),
            dma((NZ, 8)), dma((NZ, 6)), dma((NZ, 2)), dma((NZ,)),
            dma((NY, 8)), dma((NY, 6)), dma((NY, 2)), dma((NY,)),
        ],
        compiler_params=pltpu.CompilerParams(
            collective_id=0, has_side_effects=True, vmem_limit_bytes=48 * 1024 * 1024
        ),
    )(pltpu.with_memory_space_constraint(gradients, pltpu.HBM),
      pltpu.with_memory_space_constraint(step_rates, pltpu.HBM))
    return pl.pallas_call(
        finish,
        out_shape=jax.ShapeDtypeStruct(gradients.shape, F32),
        in_specs=[pl.BlockSpec(memory_space=pltpu.VMEM)] * 3,
        out_specs=pl.BlockSpec(memory_space=pl.ANY),
        scratch_shapes=[pltpu.VMEM((STEPS_HERE, EX_HERE, P_SIZE), F32), dma((STEPS_HERE // 2,))],
        compiler_params=pltpu.CompilerParams(vmem_limit_bytes=16 * 1024 * 1024),
    )(rows, last, diag)


def solution(mesh):
    in_specs = (P("step", "ex", None), P("step"))
    out_specs = P("step", "ex", None)
    return jax.shard_map(
        per_device, mesh=mesh, in_specs=in_specs, out_specs=out_specs, check_vma=False
    )
```

```python
import functools
import math

import jax
import jax.numpy as jnp
from jax import lax
from jax.experimental import pallas as pl
from jax.experimental.pallas import tpu as pltpu
from jax.sharding import PartitionSpec as P

P_SIZE = 512
BATCH = 1024
NX, NY, NZ = 4, 4, 8
STEPS_HERE = 8
EX_HERE = 128
TILE = 128
ABOVE = [(a, b) for a in range(4) for b in range(a + 1, 4)]
PAIRS = [(0, 1), (2, 3)]
PACK = 16 + (len(ABOVE) + len(PAIRS)) * TILE
PARTS = ((0, 16 + 2 * TILE),) + tuple((16 + at * TILE, 2 * TILE) for at in (2, 4, 6))
PIECE = 64
F32, BF16 = jnp.float32, jnp.bfloat16
MESH = pl.DeviceIdType.MESH


def dot_nn(a, b):
    return lax.dot_general(a, b, (((1,), (0,)), ((), ())), preferred_element_type=F32)


def dot_tn(a, b):
    return lax.dot_general(a, b, (((0,), (0,)), ((), ())), preferred_element_type=F32)


def times_rows(x_ref, column, diag, off_ref, start):
    x = x_ref[...]
    here = off_ref[pl.ds(start, x.shape[0]), :].astype(F32)
    x_ref[...] = (x * diag + column * here) + dot_nn(x.astype(BF16), off_ref[...])


def running_diags(diag_ref, count, held, start):
    product = diag_ref[0]
    held[pl.ds(0, 1), :] = product
    for s in range(1, count):
        product = product * diag_ref[s]
        held[pl.ds(s, 1), :] = product
    rows = held[:, pl.ds(start, TILE)]
    columns = jnp.concatenate([rows, jnp.zeros((TILE - rows.shape[0], TILE), F32)], axis=0).T
    return product, [columns[:, s:s + 1] for s in range(count)]


def apply_part(x_ref, diag, off_ref, at, count):
    x = x_ref[pl.ds(at, count)].reshape(count * EX_HERE, P_SIZE)
    x = x * diag + dot_nn(x.astype(BF16), off_ref[...])
    x_ref[pl.ds(at, count)] = x.reshape(count, EX_HERE, P_SIZE)


def loop(first, last, run):
    def one(i, _):
        run(i)
        return 0

    lax.fori_loop(first, last, one, 0)


def choose(k, table):
    value = table[0]
    for i in range(1, len(table)):
        value = jnp.where(k == i, table[i], value)
    return value


def body(g_hbm, rate_hbm, out_ref, last_ref, last_diag, g_ref, rate_ref, gather, stage_r, stage_l, pack, maps, diags, v,
         few, held, mine, blocks, block_diags, mine_t, lines, line_diags,
         in_sem, g_send, g_recv, st_recv, p_send, p_recv,
         b_send, b_recv, bd_send, bd_recv, t_send, t_recv, td_send, td_recv):
    step, ex = lax.axis_index("step"), lax.axis_index("ex")
    y, z = step // NZ, step % NZ
    x, c = ex // 2, ex % 2
    xr, xl, xo = (x + 1) % NX, (x + 3) % NX, (x + 2) % NX
    sib = (step, x * 2 + 1 - c)
    right, left = (step, xr * 2 + c), (step, xl * 2 + c)
    z_next, z_prev = (y * NZ + (z + 1) % NZ, ex), (y * NZ + (z + NZ - 1) % NZ, ex)
    y_next, y_prev = (((y + 1) % NY) * NZ + z, ex), (((y + NY - 1) % NY) * NZ + z, ex)

    barrier = pltpu.get_barrier_semaphore()
    peers = [sib, right, left, (step, xr * 2 + 1 - c), (step, xl * 2 + 1 - c), z_next, z_prev, y_next, y_prev]
    for peer in peers:
        pl.semaphore_signal(barrier, inc=1, device_id=peer, device_id_type=MESH)
    pl.semaphore_wait(barrier, len(peers))

    def remote(src, dst, send, recv, device):
        return pltpu.make_async_remote_copy(
            src_ref=src, dst_ref=dst, send_sem=send, recv_sem=recv, device_id=device, device_id_type=MESH
        )

    started = []

    def go(copy):
        copy.start()
        started.append(copy)

    def all_sent(count):
        for copy in started[:count]:
            copy.wait_send()
        del started[:count]

    half = EX_HERE // 2

    def send_set(core):
        n = 1 + core * 6
        step_o, step_r, step_l = xo * 2 + core, xr * 2 + core, xl * 2 + core
        go(remote(g_hbm.at[step_o, pl.ds(0, half), :], stage_r.at[core], g_send.at[n], st_recv.at[core, 0], right))
        go(remote(g_hbm.at[step_o, pl.ds(half, half), :], stage_l.at[core], g_send.at[n + 1], st_recv.at[core, 1],
                  left))
        go(remote(g_hbm.at[step_r], gather.at[ex], g_send.at[n + 2], g_recv.at[ex, 0], (step, step_r)))
        go(remote(g_hbm.at[step_l], gather.at[ex], g_send.at[n + 3], g_recv.at[ex, 0], (step, step_l)))

    def forward_set(core):
        n = 1 + core * 6
        remote(stage_r.at[core], stage_r.at[core], g_send.at[0], st_recv.at[core, 0], sib).wait_recv()
        go(remote(stage_r.at[core], gather.at[xl * 2 + c, pl.ds(0, half), :], g_send.at[n + 4],
                  g_recv.at[xl * 2 + c, 0], (step, xr * 2 + core)))
        remote(stage_l.at[core], stage_l.at[core], g_send.at[0], st_recv.at[core, 1], sib).wait_recv()
        go(remote(stage_l.at[core], gather.at[xr * 2 + c, pl.ds(half, half), :], g_send.at[n + 5],
                  g_recv.at[xr * 2 + c, 1], (step, xl * 2 + core)))

    go(remote(g_hbm.at[x * 2 + 1 - c], gather.at[ex], g_send.at[0], g_recv.at[ex, 0], sib))
    send_set(0)
    own_in = pltpu.make_async_copy(g_hbm.at[ex], gather.at[ex], in_sem.at[0])
    all_in = pltpu.make_async_copy(g_hbm, g_ref, in_sem.at[1])
    rate_in = pltpu.make_async_copy(rate_hbm, rate_ref, in_sem.at[2])
    own_in.start()
    all_in.start()
    rate_in.start()
    forward_set(0)
    send_set(1)
    own_in.wait()
    rate_in.wait()

    def gram_of(chip, first):
        rows = gather[pl.ds(chip * 2, 2)].reshape(2 * EX_HERE, P_SIZE)
        mid = P_SIZE // 2
        upper, lower = dot_tn(rows[:, :mid], rows), dot_tn(rows[:, mid:], rows[:, mid:])
        if first:
            v[:mid, :] = upper
            v[mid:, mid:] = lower
        else:
            v[:mid, :] += upper
            v[mid:, mid:] += lower

    def arrived(source):
        remote(gather.at[source], gather.at[source], g_send.at[0], g_recv.at[source, 0], sib).wait_recv()

    def arrived_half(source, which):
        part = gather.at[source, pl.ds(which * half, half), :]
        remote(part, part, g_send.at[0], g_recv.at[source, which], sib).wait_recv()

    def gram_near():
        arrived(x * 2 + 1 - c)
        gram_of(x, True)

    def gram_far():
        for at in (xr, xl):
            for core in range(2):
                arrived(at * 2 + core)
            gram_of(at, False)
        for core in range(2):
            for which in range(2):
                arrived_half(xo * 2 + core, which)
        gram_of(xo, False)

    edge = (math.sqrt(BATCH) + math.sqrt(P_SIZE)) ** 2
    scale = rate_ref[ex] / edge
    own = pack.at[ex]
    row_at = lax.broadcasted_iota(jnp.int32, (TILE, TILE), 0)
    column_at = lax.broadcasted_iota(jnp.int32, (TILE, TILE), 1)
    on, upper, lower = row_at == column_at, row_at < column_at, row_at > column_at

    def map_tile(a, b):
        return v[pl.ds(a * TILE, TILE), pl.ds(b * TILE, TILE)] * (-scale)

    def pack_part(which):
        if which == 0:
            diag_parts = []
            for a in range(4):
                d = 1.0 + jnp.sum(jnp.where(on, map_tile(a, a), 0.0), axis=0, keepdims=True)
                d_hi, d_rest = d.astype(BF16).astype(F32), d - d.astype(BF16).astype(F32)
                d_mid = d_rest.astype(BF16).astype(F32)
                diag_parts.append((d_hi, d_mid, d_rest - d_mid))
            rows = [diag_parts[a][part] for part in range(3) for a in range(4)]
            own[pl.ds(0, 16), :] = jnp.concatenate(rows + [jnp.zeros((4, TILE), F32)], axis=0).astype(BF16)
        for n in (2 * which, 2 * which + 1):
            if n < len(ABOVE):
                tile = map_tile(*ABOVE[n])
            else:
                a, b = PAIRS[n - len(ABOVE)]
                tile = jnp.where(upper, map_tile(a, a), jnp.where(lower, map_tile(b, b), 0.0))
            own[pl.ds(16 + n * TILE, TILE), :] = tile.astype(BF16)

    def packed(slot, which):
        at, size = (0, PACK) if which == 4 else PARTS[which]
        return pack.at[slot, pl.ds(at, size), :]

    p_count = [0]

    def send_pack(slot, which, device):
        n = p_count[0]
        p_count[0] += 1
        go(remote(packed(slot, which), packed(slot, which), p_send.at[n], p_recv.at[slot, which], device))

    def got_pack(slot, which):
        remote(packed(slot, which), packed(slot, which), p_send.at[0], p_recv.at[slot, which], sib).wait_recv()

    def unpack_part(slot, which):
        def put(a, b, tile):
            maps[slot, pl.ds(a * TILE, TILE), pl.ds(b * TILE, TILE)] = tile

        if which == 0:
            parts = pack[slot, pl.ds(0, 16), :].astype(F32)
            diag = parts[0:4] + (parts[4:8] + parts[8:12])
            for a in range(4):
                diags[slot, :, pl.ds(a * TILE, TILE)] = diag[a:a + 1]
        for n in (2 * which, 2 * which + 1):
            tile = pack[slot, pl.ds(16 + n * TILE, TILE), :]
            if n < len(ABOVE):
                a, b = ABOVE[n]
                put(a, b, tile)
                put(b, a, tile.T)
            else:
                a, b = PAIRS[n - len(ABOVE)]
                tile = tile.astype(F32)
                turned = tile.T
                put(a, a, jnp.where(upper, tile, turned).astype(BF16))
                put(b, b, jnp.where(lower, tile, turned).astype(BF16))

    def unpack(slot):
        for which in range(4):
            unpack_part(slot, which)

    first = []
    for which, device in ((0, left), (2, right), (1, left), (3, right), (2, left), (0, right), (3, left), (1, right),
                          (4, sib)):
        n = len(first)
        first.append(remote(packed(ex, which), packed(ex, which), p_send.at[n], p_recv.at[ex, which], device))
    p_count[0] = len(first)

    def pack_all():
        for which in range(4):
            pack_part(which)

    def send_first():
        for copy in first:
            copy.start()

    @pl.when(c == 0)
    def _():
        gram_near()
        gram_far()
        pack_all()

    @pl.when(c == 1)
    def _():
        gram_near()

    forward_set(1)

    @pl.when(c == 0)
    def _():
        send_first()

    @pl.when(c == 1)
    def _():
        gram_far()
        for which, copy in zip((0, 2, 1, 3), first):
            pack_part(which)
            copy.start()
        for copy in first[4:]:
            copy.start()

    started.extend(first)
    all_in.wait()
    from_right, from_left, across = xr * 2 + c, xl * 2 + c, xo * 2 + c
    unpack(ex)
    for s in range(STEPS_HERE):
        out_ref[s] = g_ref[s].astype(F32)

    def take(chip):
        got_pack(chip * 2 + 1 - c, 4)
        unpack(chip * 2 + 1 - c)

    @pl.when(c == 1)
    def _():
        take(x)

    for which in range(2):
        got_pack(from_right, which)
        send_pack(from_right, which, left)
        got_pack(from_left, 2 + which)
        send_pack(from_left, 2 + which, right)
    for which in range(2):
        unpack_part(from_right, which)
        unpack_part(from_left, 2 + which)
    for which in range(2):
        got_pack(from_right, 2 + which)
        got_pack(from_left, which)
    send_pack(from_right, 4, sib)
    send_pack(from_left, 4, sib)
    for which in range(2):
        unpack_part(from_right, 2 + which)
        unpack_part(from_left, which)

    @pl.when(c == 1)
    def _():
        take(xr)
        take(xl)

    for which in range(4):
        got_pack(across, which)
        send_pack(across, which, sib)
    unpack(across)

    @pl.when(c == 0)
    def _():
        take(x)
        take(xr)
        take(xl)

    for which in range(4):
        got_pack(xo * 2 + 1 - c, which)
        unpack_part(xo * 2 + 1 - c, which)

    quarters = (x % 2) * 2
    start = pl.multiple_of((c * 4 + quarters) * PIECE, 2 * PIECE)
    block_diag, columns = running_diags(diags, STEPS_HERE, held, start)
    few[...] = maps[0, pl.ds(start, 2 * PIECE), :].astype(F32)
    for s in range(1, STEPS_HERE):
        times_rows(few, columns[s - 1], diags[s], maps.at[s], start)
    block_diags[z] = block_diag
    mine[...] = few[...].astype(BF16)
    blocks[z, pl.ds(start, 2 * PIECE), :] = mine[...]

    def single(j):
        apply_part(out_ref, diags[j * 2 + 1], maps.at[j * 2 + 1], j * 2, 1)

    def unit(u):
        s = choose(u, (2, 3, 4, 4, 5, 5, 6, 6, 6, 7, 7, 7))
        pair = choose(u, (0, 0, 0, 1, 0, 1, 0, 1, 2, 0, 1, 2))
        apply_part(out_ref, diags[s], maps.at[s], pair * 2, 2)

    def later(u):
        slot = z + 1 + u // 4
        apply_part(out_ref, block_diags[slot], blocks.at[slot], (u % 4) * 2, 2)

    units = 4 * (NZ - 1 - z)

    def later_units(first, last):
        loop(jnp.minimum(first, units), jnp.minimum(last, units), later)

    early = z < NZ // 2
    inner_done = jnp.where(early, 12, 5)

    def ring(own, buf, dbuf, n, pos, ahead, behind, send, recv, d_send, d_recv, own_too, before):
        a_at = jnp.where(x == 3, 1, 0)
        to_left = jnp.where(x == 1, 0, 1)
        base = c * 4 + quarters
        p_a, p_b = base + a_at, base + 1 - a_at
        turns = n // 2

        def rows(slot, at, count):
            return buf.at[slot, pl.ds(pl.multiple_of(at * PIECE, PIECE), count * PIECE), :]

        def pass_on(slot, at, count, kind, land, device, src=None):
            there = rows(slot, at, count)
            go(remote(there if src is None else src, there, send.at[slot, kind], recv.at[slot, land], device))

        def got(slot, at, count, land):
            there = rows(slot, at, count)
            remote(there, there, send.at[slot, 0], recv.at[slot, land], sib).wait_recv()

        def pass_diag(slot, kind, device):
            go(remote(dbuf.at[slot], dbuf.at[slot], d_send.at[slot, kind], d_recv.at[slot], device))

        def got_diag(slot):
            remote(dbuf.at[slot], dbuf.at[slot], d_send.at[slot, 0], d_recv.at[slot], sib).wait_recv()

        def part(src, at):
            return None if src is None else src.at[pl.ds(pl.multiple_of(at * PIECE, PIECE), PIECE), :]

        def left_copy(slot, src=None):
            there = rows(slot, base + to_left, 1)
            mine_there = part(src, to_left)
            return remote(there if src is None else mine_there, there, send.at[slot, 5],
                          recv.at[slot, 2 + to_left], left)

        def over_a(slot, src=None):
            pass_on(slot, p_a, 1, 4, 2 + a_at, right, part(src, a_at))
            copy = left_copy(slot, src)

            @pl.when(x % 2 == 1)
            def _():
                copy.start()

            started.append(copy)

        def over_b(slot, src=None):
            copy = left_copy(slot, src)

            @pl.when(x % 2 == 0)
            def _():
                copy.start()

        def to_sibling(slot, src=None):
            pass_on(slot, base, 2, 6, 4, sib, src)

        other = c * 4 + 2 - quarters

        def over_x(slot):
            got(slot, other, 1, 2)
            got(slot, other + 1, 1, 3)
            pass_on(slot, other, 2, 7, 5, sib)

        def got_all(slot):
            got(slot, (1 - c) * 4 + quarters, 2, 4)
            got(slot, (1 - c) * 4 + 2 - quarters, 2, 5)

        own_a, own_b = part(own, a_at), part(own, 1 - a_at)
        pass_on(pos, p_a, 1, 0, 0, ahead, own_a)
        pass_on(pos, p_b, 1, 3, 1, behind, own_b)
        pass_on(pos, p_b, 1, 1, 1, ahead, own_b)
        pass_on(pos, p_a, 1, 2, 0, behind, own_a)
        pass_diag(pos, 0, ahead)
        pass_diag(pos, 1, behind)
        if own_too:
            over_a(pos, own)
            over_b(pos, own)
            to_sibling(pos, own)

        waiting = [pos] if own_too else []
        for s in range(turns):
            last = s == turns - 1
            up, down = (pos + n - 1 - s) % n, (pos + 1 + s) % n
            before[s](got_all)
            got(up, p_a, 1, 0)
            if not last:
                pass_on(up, p_a, 1, 0, 0, ahead)
            over_a(up)
            got(down, p_b, 1, 1)
            if not last:
                pass_on(down, p_b, 1, 3, 1, behind)
            over_b(down)
            if last:
                to_sibling(up)
            else:
                got(up, p_b, 1, 1)
                if s < turns - 2:
                    pass_on(up, p_b, 1, 1, 1, ahead)
                over_b(up)
                got(down, p_a, 1, 0)
                if s < turns - 2:
                    pass_on(down, p_a, 1, 2, 0, behind)
                over_a(down)
                to_sibling(up)
                to_sibling(down)
            got_diag(up)
            if not last:
                pass_diag(up, 0, ahead)
                got_diag(down)
                if s < turns - 2:
                    pass_diag(down, 1, behind)
            for slot in waiting:
                over_x(slot)
            waiting = [up] if last else [up, down]
        before[turns](got_all)
        for slot in waiting:
            over_x(slot)

        return got_all

    before_ring = len(started)

    def first_fill(got_all):
        loop(0, STEPS_HERE // 2, single)
        loop(0, inner_done, unit)

    def block_fill(got_all):
        for d in (1, 2):
            got_all((z + d) % NZ)

            @pl.when(early)
            def _():
                loop(4 * d - 4, 4 * d, later)

    def last_fill(got_all):
        all_sent(before_ring)
        got_all((z + 3) % NZ)
        for d in (0, 5, 6, 7):
            got_all((z + d) % NZ)

        @pl.when(early)
        def _():
            loop(8, 12, later)

    got_all = ring(mine, blocks, block_diags, NZ, z, z_next, z_prev, b_send, b_recv, bd_send, bd_recv, True,
                   [first_fill, lambda _: None, lambda _: None, block_fill, last_fill])

    farthest = (z + NZ // 2) % NZ
    line_diag, columns = running_diags(block_diags, NZ, held, start)

    @pl.when(z >= NZ // 2)
    def _():
        got_all(farthest)

    few[...] = blocks[0, pl.ds(start, 2 * PIECE), :].astype(F32)
    for s in range(1, NZ // 2):
        times_rows(few, columns[s - 1], block_diags[s], blocks.at[s], start)

    @pl.when(early)
    def _():
        got_all(farthest)

    for s in range(NZ // 2, NZ):
        times_rows(few, columns[s - 1], block_diags[s], blocks.at[s], start)
    line_diags[y] = line_diag
    mine_t[...] = few[...].astype(BF16)

    done = jnp.where(early, 12, 0)
    before_line = len(started)

    def line_fill(got_all):
        loop(inner_done, 12, unit)
        later_units(done, done + 8)

    got_all = ring(mine_t, lines, line_diags, NY, y, y_next, y_prev, t_send, t_recv, td_send, td_recv, False,
                   [line_fill, lambda _: later_units(done + 8, done + 12), lambda _: all_sent(before_line)])
    later_units(done + 12, done + 28)

    for d in range(1, NY):
        slot = (y + d) % NY
        got_all(slot)

        @pl.when(y + d < NY - 1)
        def _():
            for at in (0, 4):
                apply_part(out_ref, line_diags[slot], lines.at[slot], at, 4)

    @pl.when(y < NY - 1)
    def _():
        last_ref[...] = lines[NY - 1]
        last_diag[...] = line_diags[NY - 1]

    @pl.when(y == NY - 1)
    def _():
        last_ref[...] = jnp.zeros_like(last_ref)
        last_diag[...] = jnp.ones_like(last_diag)

    all_sent(len(started))


def finish(x_ref, off_ref, diag_ref, out_hbm, held, sem):
    copies = []
    for i in range(STEPS_HERE // 2):
        x = x_ref[pl.ds(i * 2, 2)].reshape(2 * EX_HERE, P_SIZE)
        x = x * diag_ref[...] + dot_nn(x.astype(BF16), off_ref[...])
        held[pl.ds(i * 2, 2)] = x.reshape(2, EX_HERE, P_SIZE)
        copies.append(pltpu.make_async_copy(held.at[pl.ds(i * 2, 2)], out_hbm.at[pl.ds(i * 2, 2)], sem.at[i]))
        copies[-1].start()
    for copy in copies:
        copy.wait()


def per_device(gradients, step_rates):
    square = (P_SIZE, P_SIZE)
    dma = pltpu.SemaphoreType.DMA
    rows, last, diag = pl.pallas_call(
        body,
        out_shape=[jax.ShapeDtypeStruct(gradients.shape, F32), jax.ShapeDtypeStruct(square, BF16),
                   jax.ShapeDtypeStruct((1, P_SIZE), F32)],
        in_specs=[pl.BlockSpec(memory_space=pl.ANY)] * 2,
        out_specs=[pl.BlockSpec(memory_space=pltpu.VMEM)] * 3,
        scratch_shapes=[
            pltpu.VMEM((STEPS_HERE, EX_HERE, P_SIZE), BF16),
            pltpu.SMEM((STEPS_HERE,), F32),
            pltpu.VMEM((8, EX_HERE, P_SIZE), BF16),
            pltpu.VMEM((2, EX_HERE // 2, P_SIZE), BF16),
            pltpu.VMEM((2, EX_HERE // 2, P_SIZE), BF16),
            pltpu.VMEM((STEPS_HERE, PACK, TILE), BF16),
            pltpu.VMEM((STEPS_HERE,) + square, BF16),
            pltpu.VMEM((STEPS_HERE, 1, P_SIZE), F32),
            pltpu.VMEM(square, F32),
            pltpu.VMEM((2 * PIECE, P_SIZE), F32),
            pltpu.VMEM((8, P_SIZE), F32),
            pltpu.VMEM((2 * PIECE, P_SIZE), BF16),
            pltpu.VMEM((NZ,) + square, BF16),
            pltpu.VMEM((NZ, 1, P_SIZE), F32),
            pltpu.VMEM((2 * PIECE, P_SIZE), BF16),
            pltpu.VMEM((NY,) + square, BF16),
            pltpu.VMEM((NY, 1, P_SIZE), F32),
            dma((3,)),
            dma((13,)), dma((8, 2)), dma((2, 2)), dma((19,)), dma((8, 5)),
            dma((NZ, 8)), dma((NZ, 6)), dma((NZ, 2)), dma((NZ,)),
            dma((NY, 8)), dma((NY, 6)), dma((NY, 2)), dma((NY,)),
        ],
        compiler_params=pltpu.CompilerParams(
            collective_id=0, has_side_effects=True, vmem_limit_bytes=48 * 1024 * 1024
        ),
    )(pltpu.with_memory_space_constraint(gradients, pltpu.HBM),
      pltpu.with_memory_space_constraint(step_rates, pltpu.HBM))
    return pl.pallas_call(
        finish,
        out_shape=jax.ShapeDtypeStruct(gradients.shape, F32),
        in_specs=[pl.BlockSpec(memory_space=pltpu.VMEM)] * 3,
        out_specs=pl.BlockSpec(memory_space=pl.ANY),
        scratch_shapes=[pltpu.VMEM((STEPS_HERE, EX_HERE, P_SIZE), F32), dma((STEPS_HERE // 2,))],
        compiler_params=pltpu.CompilerParams(vmem_limit_bytes=16 * 1024 * 1024),
    )(rows, last, diag)


def solution(mesh):
    in_specs = (P("step", "ex", None), P("step"))
    out_specs = P("step", "ex", None)
    return jax.shard_map(
        per_device, mesh=mesh, in_specs=in_specs, out_specs=out_specs, check_vma=False
    )
```
